256 devices in a mesh: grp: 16 (over z, core), wide: 16 (over y, x).
Axes of the slice: x: 4, y: 4, z: 8, core: 2. Of those that a mesh axis runs over, the one named last changes fastest.
Arguments:
- embeddings: bfloat16 [131072, 4096], P(('grp', 'wide')), may hold values from -6 to 6
- worker_of_row: int32 [131072, 1], P(('grp', 'wide')), may hold values from 0 to 255, as said below
Outputs:
- max_similarity: float32 [131072], P(('grp', 'wide'))
The draws below stay inside these ranges and needn't reach their ends.
Inputs may be any that keep to these rules, and one draw needn't show every extreme that they name: `worker_of_row`: in the rows of one device no cluster is named more than 4 times; one cluster is named exactly 4 times by the rows of every device, and another is named by exactly one row in all.
All inputs are finite; a program needn't handle non-finite values.
Results may differ from the reference program's by a relative error of at most 0.0014.
Values may be sent and summed in bfloat16 or wider, within the bound.
No kernel may reach another device: no remote copies, remote signals or barrier semaphores. Data moves between devices by JAX's collectives and lax.ppermute only.
A program may use at most 128 MiB of HBM per device.

```python
import jax
import jax.numpy as jnp
from jax import lax

D = 4096
ROWS_DEV = 512
WORKERS = 256
CAP = 4
ROWS = 131072


def draw_worker_of_row(key, part):
    key = jax.random.fold_in(key, 11)
    slot_total = WORKERS * CAP
    keys_all = jax.random.split(key, 6)
    pick_key = keys_all[0]
    offset_key = keys_all[1]
    source_key = keys_all[2]
    bias_key = keys_all[3]
    jitter_key = keys_all[4]
    order_key = keys_all[5]
    full_worker = jax.random.randint(pick_key, (), 0, WORKERS)
    lone_offset = jax.random.randint(offset_key, (), 1, WORKERS)
    lone_worker = (full_worker + lone_offset) % WORKERS
    lone_source = jax.random.randint(source_key, (), 0, WORKERS)
    worker_bias = jax.random.randint(bias_key, (WORKERS,), 0, 4096)
    slot_ids = jnp.arange(slot_total)
    slot_worker = slot_ids // CAP
    slot_rank = slot_ids % CAP

    def one_source(source):
        jitter = jax.random.randint(jax.random.fold_in(jitter_key, source), (slot_total,), 0, 4096)
        priority = worker_bias[slot_worker] + jitter
        priority = jnp.where(slot_worker == full_worker, 16384, priority)
        lone_here = slot_worker == lone_worker
        keep_one = lone_here & (slot_rank == 0) & (source == lone_source)
        priority = jnp.where(lone_here, jnp.where(keep_one, 16384, -1), priority)
        ranking = priority * slot_total + slot_ids
        chosen = lax.top_k(ranking, ROWS_DEV)[1]
        picked = chosen // CAP
        return jax.random.permutation(jax.random.fold_in(order_key, source), picked)
    assigned = jax.vmap(one_source)(jnp.arange(WORKERS))
    return assigned.reshape(ROWS, 1).astype(jnp.int32)


def steps_of(rng, shape, cuts, least, high):
    factor_of = 1.0
    for position, parts in cuts:
        draws = jax.random.uniform(jax.random.fold_in(jax.random.fold_in(rng, 6), position), (parts,), jnp.float32, least / len(cuts), high / len(cuts))
        factor_of = factor_of * jnp.repeat(jnp.exp(draws), shape[position] // parts).reshape((-1,) + (1,) * (len(shape) - 1 - position))
    return factor_of


def gaussian(stream_key, shape, scale, limit, pieces=(), held_as=jnp.bfloat16):
    values = scale * jax.random.normal(stream_key, shape, jnp.float32)
    if pieces:
        values = values * steps_of(stream_key, shape, pieces, -0.22, 0.18)
    return jnp.clip(values, -limit, limit).astype(held_as)


def setup_inputs(seed: int = 0) -> dict:
    keys = jax.random.split(jax.random.key(seed), 3)
    embeddings = gaussian(keys[0], (ROWS, D), 1.0, 6.0, ((0, 256),))
    worker_of_row = draw_worker_of_row(jax.random.fold_in(keys[2], 71), 0)
    return {"embeddings": embeddings, "worker_of_row": worker_of_row}


def reference(embeddings, worker_of_row):
    values = embeddings.astype(jnp.float32)
    spread = lax.optimization_barrier(jnp.mean(values * values, axis=1, keepdims=True))
    scaled = (values * lax.rsqrt(spread + 1e-06) * D ** (-0.25)).astype(jnp.bfloat16)
    cluster_key = worker_of_row[:, 0].astype(jnp.int32)
    ordering = jnp.argsort(cluster_key, stable=True).astype(jnp.int32)
    sorted_key = cluster_key[ordering]
    sorted_rows = scaled[ordering]
    cluster_start = jnp.searchsorted(sorted_key, sorted_key, side='left').astype(jnp.int32)
    cluster_end = jnp.searchsorted(sorted_key, sorted_key, side='right').astype(jnp.int32)
    tile_rows = 128
    block_rows = 512
    padded_rows = jnp.concatenate([sorted_rows, jnp.zeros((block_rows, D), jnp.bfloat16)], axis=0)
    padded_key = jnp.concatenate([sorted_key, jnp.full((block_rows,), -1, jnp.int32)], axis=0)

    def compare_tile(tile_index):
        first_row = (tile_index * tile_rows).astype(jnp.int32)
        span_low = cluster_start[first_row]
        span_high = cluster_end[first_row + tile_rows - 1]
        queries = lax.dynamic_slice(sorted_rows, (first_row, jnp.int32(0)), (tile_rows, D))
        query_key = lax.dynamic_slice(sorted_key, (first_row,), (tile_rows,))
        query_pos = first_row + jnp.arange(tile_rows).astype(jnp.int32)
        blocks = ((span_high - span_low + block_rows - 1) // block_rows).astype(jnp.int32)

        def advance(carry_state):
            counter, running = carry_state
            block_start = (span_low + counter * block_rows).astype(jnp.int32)
            others = lax.dynamic_slice(padded_rows, (block_start, jnp.int32(0)), (block_rows, D))
            other_key = lax.dynamic_slice(padded_key, (block_start,), (block_rows,))
            other_pos = block_start + jnp.arange(block_rows).astype(jnp.int32)
            scores = jnp.dot(queries, others.T, preferred_element_type=jnp.float32)
            paired = (query_key[:, None] == other_key[None, :]) & (query_pos[:, None] != other_pos[None, :])
            running = jnp.maximum(running, lax.optimization_barrier(jnp.max(jnp.where(paired, scores, -1e+30), axis=1)))
            return ((counter + 1).astype(jnp.int32), running)

        def unfinished(carry_state):
            return carry_state[0] < blocks
        initial = (jnp.int32(0), jnp.full((tile_rows,), -1e+30, jnp.float32))
        return lax.while_loop(unfinished, advance, initial)[1]
    tile_best = lax.map(compare_tile, jnp.arange(ROWS // tile_rows).astype(jnp.int32)).reshape(ROWS)
    result = jnp.zeros((ROWS,), jnp.float32).at[ordering].set(tile_best)
    return jnp.where(result > -1e+29, result, 0.0).astype(jnp.float32)
```

```python
import functools

import jax
import jax.numpy as jnp
from jax import lax
from jax.experimental import pallas as pl
from jax.experimental.pallas import tpu as pltpu
from jax.sharding import PartitionSpec as P

GRP = ("z", "core")
CORE_WIDE = ("core", "wide")
ALL = ("z", "core", "wide")
PLANES = 8
WIDE = 16
PER_PLANE = 32
WORKERS = 256
CAP = 4
HALF = 512
OUT = 1024
CAPS = (256, 192, 128, 64)
LIST = CAPS[0]
OWN_LIST = 128
Z_FIRST = (1536, 1536)
WIDE_FIRST = 1024
MARK = 2.0
REAL_MAX = 100.0
TILE = 512
ROW_TILE = 256
VMEM_LIMIT = 56 * 2**20


def padded_plan(embeddings, worker_of_row):
    row_count, features = embeddings.shape
    grp_count = lax.axis_size("z") * lax.axis_size("core")
    wide_count = lax.axis_size("wide")
    workers = grp_count * wide_count
    slot_count = workers * CAP
    values = embeddings.astype(jnp.float32)
    spread = jnp.mean(values * values, axis=1, keepdims=True)
    scaled = (values * lax.rsqrt(spread + 1e-06) * features ** (-0.25)).astype(jnp.bfloat16)
    target = worker_of_row[:, 0]
    matches = target[:, None] == jnp.arange(workers, dtype=jnp.int32)[None, :]
    one_hot = matches.astype(jnp.bfloat16)
    row_ids = jnp.arange(row_count, dtype=jnp.int32)
    earlier_mask = (row_ids[:, None] > row_ids[None, :]).astype(jnp.bfloat16)
    earlier = jnp.dot(earlier_mask, one_hot, preferred_element_type=jnp.float32)
    slot_index = jnp.sum(jnp.where(matches, earlier, 0.0), axis=1).astype(jnp.int32)
    sent_counts = jnp.sum(matches.astype(jnp.int32), axis=0)
    position = target * CAP + slot_index
    outgoing = jnp.zeros((slot_count, features), jnp.bfloat16).at[position].set(scaled)
    outgoing = outgoing.reshape(grp_count, wide_count, CAP, features)
    sent_counts = sent_counts.reshape(grp_count, wide_count, 1)

    def there(value):
        value = lax.all_to_all(value, GRP, split_axis=0, concat_axis=0, tiled=True)
        return lax.all_to_all(value, "wide", split_axis=1, concat_axis=1, tiled=True)

    arrived = there(outgoing).reshape(slot_count, features)
    counts_each = jnp.repeat(there(sent_counts).reshape(workers), CAP)
    slot_ids = jnp.arange(slot_count, dtype=jnp.int32)
    filled = slot_ids % CAP < counts_each
    paired = filled[:, None] & filled[None, :] & (slot_ids[:, None] != slot_ids[None, :])
    scores = lax.dot_general(
        arrived, arrived, (((1,), (1,)), ((), ())), preferred_element_type=jnp.float32
    )
    highest = jnp.max(jnp.where(paired, scores, -1e30), axis=1)
    back = highest.reshape(grp_count, wide_count, CAP)
    back = lax.all_to_all(back, "wide", split_axis=1, concat_axis=1, tiled=True)
    back = lax.all_to_all(back, GRP, split_axis=0, concat_axis=0, tiled=True)
    own_best = back.reshape(slot_count)[position]
    return jnp.where(own_best > -1e29, own_best, 0.0)


def z_shift(step):
    return [(z, (z + step) % PLANES) for z in range(PLANES)]


def after(value, *others):
    return lax.optimization_barrier((value,) + others)[0]


def call(kernel, out_shape, flops, **settings):
    return pl.pallas_call(
        kernel,
        out_shape=out_shape,
        compiler_params=pltpu.CompilerParams(vmem_limit_bytes=VMEM_LIMIT),
        cost_estimate=pl.CostEstimate(
            flops=flops, bytes_accessed=8 * 2**20, transcendentals=0
        ),
        **settings,
    )


def whole(value):
    return pl.BlockSpec(value.shape, lambda i: (0,) * value.ndim)


def columns(rows, first=0):
    return pl.BlockSpec((rows, TILE), lambda i: (0, first + i))


def scaled_rows(x_ref, scale_ref):
    return (x_ref[...].astype(jnp.float32) * scale_ref[...]).astype(jnp.bfloat16)


def pack_kernel(pick_ref, fill_ref, note_ref, scale_ref, x_ref, *out_refs):
    packed = jnp.dot(
        pick_ref[...], scaled_rows(x_ref, scale_ref), preferred_element_type=jnp.float32
    )
    packed = (packed + fill_ref[...] * note_ref[...]).astype(jnp.bfloat16)
    base = 0
    for out_ref in out_refs:
        rows = out_ref.shape[0]
        out_ref[...] = packed[base : base + rows, :]
        base += rows


def pack(pick, fill, note, scale, embeddings, first_column, parts):
    width = note.shape[1]
    return call(
        pack_kernel,
        [jax.ShapeDtypeStruct((rows, width), jnp.bfloat16) for rows in parts],
        2 * pick.shape[0] * HALF * width,
        grid=(width // TILE,),
        in_specs=[
            whole(pick),
            whole(fill),
            columns(1),
            whole(scale),
            columns(HALF, first_column // TILE),
        ],
        out_specs=[columns(rows) for rows in parts],
    )(pick, fill, note, scale, embeddings)


def reorder_kernel(pick_ref, x_ref, *out_refs):
    moved = jnp.dot(pick_ref[...], x_ref[...], preferred_element_type=jnp.float32)
    moved = moved.astype(jnp.bfloat16)
    for index, out_ref in enumerate(out_refs):
        out_ref[...] = moved[index * 128 : index * 128 + 128, :]


def reorder(pick, value):
    width = value.shape[1]
    return call(
        reorder_kernel,
        [jax.ShapeDtypeStruct((128, width), jnp.bfloat16)] * PLANES,
        2 * OUT * OUT * width,
        grid=(width // TILE,),
        in_specs=[whole(pick), columns(OUT)],
        out_specs=[columns(128)] * PLANES,
    )(pick, value)


def repack_kernel(pick_ref, *refs):
    blocks, out_ref, held = refs[:-2], refs[-2], refs[-1]
    base = 0
    for block in blocks:
        rows = block.shape[0]
        held[base : base + rows, :] = block[...]
        base += rows
    out_ref[...] = jnp.dot(
        pick_ref[...], held[...], preferred_element_type=jnp.float32
    ).astype(jnp.bfloat16)


def repack(pick, blocks):
    depth = pick.shape[1]
    width = blocks[0].shape[1]
    return call(
        repack_kernel,
        jax.ShapeDtypeStruct((OUT, width), jnp.bfloat16),
        2 * OUT * depth * width,
        grid=(width // TILE,),
        in_specs=[whole(pick)] + [columns(block.shape[0]) for block in blocks],
        out_specs=columns(OUT),
        scratch_shapes=[pltpu.VMEM((depth, TILE), jnp.bfloat16)],
    )(pick, *blocks)


def gram_kernel(has_total, *refs):
    if has_total:
        total_ref, pick_ref, x_ref, out_ref, held = refs
    else:
        pick_ref, x_ref, out_ref, held = refs
    step = pl.program_id(0)
    moved = jnp.dot(pick_ref[...], x_ref[...], preferred_element_type=jnp.float32)
    held[step] = moved.astype(jnp.bfloat16)

    @pl.when(step == pl.num_programs(0) - 1)
    def _():
        for tile in range(0, OUT, ROW_TILE):
            part = total_ref[tile : tile + ROW_TILE, :] if has_total else 0.0
            for index in range(held.shape[0]):
                part = part + lax.dot_general(
                    held[index, tile : tile + ROW_TILE, :],
                    held[index],
                    (((1,), (1,)), ((), ())),
                    preferred_element_type=jnp.float32,
                )
            out_ref[tile : tile + ROW_TILE, :] = part


def gram(total, pick, value):
    width = value.shape[1]
    first = [] if total is None else [total]
    return call(
        functools.partial(gram_kernel, total is not None),
        jax.ShapeDtypeStruct((OUT, OUT), jnp.float32),
        4 * OUT * OUT * width,
        grid=(width // TILE,),
        in_specs=[whole(operand) for operand in first] + [whole(pick), columns(OUT)],
        out_specs=pl.BlockSpec((OUT, OUT), lambda i: (0, 0)),
        scratch_shapes=[pltpu.VMEM((width // TILE, OUT, TILE), jnp.bfloat16)],
    )(*first, pick, value)


def best_kernel(total_ref, *refs):
    blocks, out_ref, held, scores = refs[:PLANES], refs[PLANES], refs[-2], refs[-1]
    for index, block in enumerate(blocks):
        held[index * 128 : index * 128 + 128, :] = block[...]
    best = jnp.full((1, OUT), -1e30, jnp.float32)
    for tile in range(0, OUT, ROW_TILE):
        scores[tile : tile + ROW_TILE, :] = total_ref[tile : tile + ROW_TILE, :] + lax.dot_general(
            held[tile : tile + ROW_TILE, :],
            held[...],
            (((1,), (1,)), ((), ())),
            preferred_element_type=jnp.float32,
        )
    for tile in range(0, OUT, ROW_TILE):
        part = scores[tile : tile + ROW_TILE, :]
        row = tile + lax.broadcasted_iota(jnp.int32, (ROW_TILE, OUT), 0)
        column = lax.broadcasted_iota(jnp.int32, (ROW_TILE, OUT), 1)
        same = row == column
        squares = jnp.sum(jnp.where(same, part, 0.0), axis=1, keepdims=True)
        open_pair = jnp.logical_not(same) & (squares < REAL_MAX)
        best = jnp.maximum(
            best, jnp.max(jnp.where(open_pair, part, -1e30), axis=0, keepdims=True)
        )
    out_ref[...] = jnp.where(best > -1e29, best, 0.0)


def best_of(total, blocks):
    width = blocks[0].shape[1]
    vmem = pl.BlockSpec(memory_space=pltpu.VMEM)
    return call(
        best_kernel,
        jax.ShapeDtypeStruct((1, OUT), jnp.float32),
        2 * OUT * OUT * width,
        in_specs=[vmem] * (1 + PLANES),
        out_specs=vmem,
        scratch_shapes=[
            pltpu.VMEM((OUT, width), jnp.bfloat16),
            pltpu.VMEM((OUT, OUT), jnp.float32),
        ],
    )(total, *blocks)


def on_device(embeddings, worker_of_row):
    i32 = jnp.int32
    rows = embeddings.shape[0]
    z = lax.axis_index("z")
    core = lax.axis_index("core")
    wide = lax.axis_index("wide")

    target = worker_of_row[:, 0]
    clusters = jnp.arange(WORKERS, dtype=i32)
    matches = target[:, None] == clusters[None, :]
    one_hot = matches.astype(jnp.bfloat16)
    row_ids = jnp.arange(rows, dtype=i32)
    earlier_mask = (row_ids[:, None] > row_ids[None, :]).astype(jnp.bfloat16)
    earlier = jnp.dot(earlier_mask, one_hot, preferred_element_type=jnp.float32)
    counts = jnp.sum(matches.astype(jnp.float32), axis=0)
    same_plane = clusters[:, None] // PER_PLANE == clusters[None, :] // PER_PLANE
    ahead = jnp.sum(
        jnp.where(same_plane & (clusters[:, None] < clusters[None, :]), counts[:, None], 0.0), axis=0
    )
    rank = jnp.sum(jnp.where(matches, earlier, 0.0), axis=1).astype(i32)
    place = jnp.sum(jnp.where(matches, earlier + ahead[None, :], 0.0), axis=1).astype(i32)
    distance = (target // PER_PLANE - z) % PLANES
    cluster_distance = (clusters // PER_PLANE - z) % PLANES
    n = [
        jnp.sum(jnp.where(cluster_distance == d, counts, 0.0)).astype(i32) for d in range(PLANES)
    ]
    low = functools.reduce(
        jnp.maximum,
        (
            0,
            n[4] - CAPS[3] + 1,
            n[4] + n[5] - CAPS[2] + 1,
            n[4] + n[5] + n[6] - CAPS[1] + 1,
            n[4] + n[5] + n[6] + n[7] - CAPS[0] + 1,
        ),
    )
    high = functools.reduce(
        jnp.minimum,
        (
            n[4],
            CAPS[3] - 1,
            CAPS[2] - 1 - n[3],
            CAPS[1] - 1 - n[3] - n[2],
            CAPS[0] - 1 - n[3] - n[2] - n[1],
        ),
    )
    overflow = (low > high).astype(i32)
    to_right = jnp.clip((low + high) // 2, 0, n[4])
    starts = [
        jnp.int32(0),
        to_right + n[3] + n[2],
        to_right + n[3],
        to_right,
        to_right,
        n[4] - to_right,
        n[4] - to_right + n[5],
        n[4] - to_right + n[5] + n[6],
    ]

    def by_distance(which):
        value = jnp.zeros(which.shape, i32)
        for d in range(1, PLANES):
            value = jnp.where(which == d, starts[d], value)
        return value

    start = by_distance(distance)
    far = distance == 4
    right_place = jnp.where(
        (distance >= 1) & (distance <= 3),
        start + place,
        jnp.where(far & (place < to_right), place, -1),
    )
    left_place = jnp.where(
        distance >= 5,
        start + place,
        jnp.where(far & (place >= to_right), place - to_right, -1),
    )
    list_ids = jnp.arange(2 * LIST + OWN_LIST, dtype=i32)
    list_place = jnp.where(
        distance == 0,
        2 * LIST + place,
        jnp.where(
            (right_place >= 0) & (right_place < LIST - 1),
            1 + right_place,
            jnp.where(
                (left_place >= 0) & (left_place < LIST - 1), LIST + 1 + left_place, -1
            ),
        ),
    )
    list_pick = (list_place[None, :] == list_ids[:, None]).astype(jnp.bfloat16)
    list_fill = ((list_ids == 0) | (list_ids == LIST)).astype(jnp.float32)[:, None]
    values = embeddings.astype(jnp.float32)
    spread = jnp.mean(values * values, axis=1, keepdims=True)
    scale = lax.rsqrt(spread + 1e-06) * embeddings.shape[1] ** (-0.25)
    column = target % WIDE
    slot_ids = jnp.arange(OUT, dtype=i32)

    cluster_start = by_distance(cluster_distance).astype(jnp.float32)
    told = jnp.concatenate([counts, ahead, cluster_start])
    first_note = jnp.pad(told, (0, Z_FIRST[0] - told.shape[0]))[None, :]
    notes = (first_note,) + tuple(jnp.zeros((1, width), jnp.float32) for width in Z_FIRST[1:])

    wide_place = (target // WIDE % 2) * HALF + column * 32 + distance * CAP + rank
    wide_match = wide_place[None, :] == slot_ids[:, None]
    wide_fill = 1.0 - jnp.sum(wide_match.astype(jnp.float32), axis=1, keepdims=True)
    wide_rows = pack(
        wide_match.astype(jnp.bfloat16),
        wide_fill,
        jnp.full((1, WIDE_FIRST), MARK, jnp.float32),
        scale,
        embeddings,
        sum(Z_FIRST),
        (OUT,),
    )[0]
    wide_back = lax.all_to_all(wide_rows, CORE_WIDE, 0, 0, tiled=True)
    final = slot_ids[:, None]
    step_of, core_of, column_of = final // 128, final // 64 % 2, final // 4 % WIDE
    final_from = core_of * HALF + column_of * 32 + step_of * CAP + final % CAP
    final_order = (final_from == slot_ids[None, :]).astype(jnp.bfloat16)
    wide_blocks = reorder(final_order, wide_back)

    right_steps, left_steps = z_shift(1), z_shift(-1)
    got, own = [], []
    first_columns = (0, Z_FIRST[0])
    for f, width in enumerate(Z_FIRST):
        right, left, mine = pack(
            list_pick,
            list_fill,
            notes[f],
            scale,
            embeddings,
            first_columns[f],
            (LIST, LIST, OWN_LIST),
        )
        if f > 0:
            right, left = after(right, got[0][2]), after(left, got[0][6])
        rights, lefts = [], []
        for hop in range(4):
            if hop > 0:
                right, left = rights[-1][: CAPS[hop]], lefts[-1][: CAPS[hop]]
            if f == 0 and hop == 1:
                right, left = after(right, wide_rows), after(left, wide_rows)
            if f == 1 and hop == 1:
                right, left = after(right, wide_back), after(left, wide_back)
            rights.append(lax.ppermute(right, "z", right_steps))
            lefts.append(lax.ppermute(left, "z", left_steps))
        got.append(rights + lefts)
        own.append(mine)

    gates = {1: 0, 7: 0, 2: 1, 6: 1, 3: 2, 5: 2, 4: 3}
    last_blocks = [wide_blocks[0]] + [None] * 7
    for step, hop in gates.items():
        block = after(wide_blocks[step], got[1][hop], got[1][4 + hop])
        last_blocks[step] = lax.ppermute(block, "z", z_shift(step))

    blocks = got[0]
    heard = jnp.concatenate(
        [
            told[None, :],
            *[blocks[b][0:1, : told.shape[0]].astype(jnp.float32) for b in (0, 1, 2, 3, 6, 5, 4)],
        ]
    ).astype(i32)
    heard = heard.reshape(PLANES, 3, PLANES, PER_PLANE)
    plane_ids = jnp.arange(PLANES, dtype=i32)
    heard = jnp.sum(jnp.where(plane_ids[:, None] == z, heard, 0), axis=2)
    heard = heard.reshape(PLANES, 3, 2, WIDE).transpose(1, 2, 3, 0)[..., None]
    slot_count, slot_place, slot_start = heard[0], heard[1], heard[2]
    ranks = jnp.arange(CAP, dtype=i32)
    slot_place = slot_place + ranks
    offsets = [OWN_LIST]
    for cap in CAPS + CAPS:
        offsets.append(offsets[-1] + cap)
    depth = offsets[-1]
    steps = plane_ids[:, None]
    block_base = jnp.array(
        [0]
        + [offsets[b] + 1 for b in (0, 1, 2, 3, 6, 5, 4)],
        dtype=i32,
    )[:, None]
    slot_from = jnp.where(
        steps == 0,
        slot_place,
        jnp.where(
            steps == 4,
            jnp.where(
                slot_place < slot_start,
                offsets[3] + 1 + slot_place,
                offsets[7] + 1 + slot_place - slot_start,
            ),
            block_base + slot_start + slot_place,
        ),
    )
    slot_from = jnp.where(ranks < slot_count, slot_from, -1).reshape(OUT)
    depth_ids = jnp.arange(depth, dtype=i32)
    slot_pick = (slot_from[:, None] == depth_ids[None, :]).astype(jnp.bfloat16)

    scores = None
    last_wide = wide_back
    for f in range(len(Z_FIRST)):
        packed = repack(slot_pick, [own[f]] + got[f])
        arrived = lax.all_to_all(after(packed, last_wide), CORE_WIDE, 0, 0, tiled=True)
        scores = gram(scores, final_order, arrived)
        last_wide = arrived
    best = best_of(scores, last_blocks)

    best = jnp.where(overflow > 0, 1e30, best.reshape(PLANES, 128))
    step_to = (z - plane_ids) % PLANES
    best = jnp.sum(
        jnp.where(step_to[:, None, None] == plane_ids[None, :, None], best[None], 0.0), axis=1
    )
    best = jnp.broadcast_to(best[:, None, None], (PLANES, 2 * WIDE, 1, 128))
    back = lax.all_to_all(best.reshape(WORKERS, 1, 128), ALL, 0, 0, tiled=True)
    back = back.reshape(WORKERS, 128)
    failed = jnp.max(back) > 1e29
    mine = lax.dynamic_slice(back, (0, core * 64 + wide * CAP), (WORKERS, CAP))
    result = jnp.sum(
        jnp.where(
            (target * CAP + rank)[None, :] == slot_ids[:, None],
            mine.reshape(OUT)[:, None],
            0.0,
        ),
        axis=0,
    )
    return lax.cond(failed, padded_plan, lambda *_: result, embeddings, worker_of_row)


def solution(mesh):
    split = jax.sharding.Mesh(mesh.devices.reshape(PLANES, 2, WIDE), ALL)
    placed = (P(ALL, None), P(ALL, None))
    return jax.shard_map(
        on_device, mesh=split, in_specs=placed, out_specs=P(ALL), check_vma=False
    )
```

```python
import functools

import jax
import jax.numpy as jnp
from jax import lax
from jax.experimental import pallas as pl
from jax.experimental.pallas import tpu as pltpu
from jax.sharding import PartitionSpec as P

GRP = ("z", "core")
CORE_WIDE = ("core", "wide")
ALL = ("z", "core", "wide")
PLANES = 8
WIDE = 16
PER_PLANE = 32
WORKERS = 256
CAP = 4
HALF = 512
OUT = 1024
CAPS = (256, 192, 128, 64)
LIST = CAPS[0]
OWN_LIST = 128
Z_FIRST = (1280, 1024)
WIDE_FIRST = 1792
MARK = 2.0
REAL_MAX = 100.0
ROW_TILE = 256
NOTE = 1280
VMEM_LIMIT = 56 * 2**20


def padded_plan(embeddings, worker_of_row):
    row_count, features = embeddings.shape
    grp_count = lax.axis_size("z") * lax.axis_size("core")
    wide_count = lax.axis_size("wide")
    workers = grp_count * wide_count
    slot_count = workers * CAP
    values = embeddings.astype(jnp.float32)
    spread = jnp.mean(values * values, axis=1, keepdims=True)
    scaled = (values * lax.rsqrt(spread + 1e-06) * features ** (-0.25)).astype(jnp.bfloat16)
    target = worker_of_row[:, 0]
    matches = target[:, None] == jnp.arange(workers, dtype=jnp.int32)[None, :]
    one_hot = matches.astype(jnp.bfloat16)
    row_ids = jnp.arange(row_count, dtype=jnp.int32)
    earlier_mask = (row_ids[:, None] > row_ids[None, :]).astype(jnp.bfloat16)
    earlier = jnp.dot(earlier_mask, one_hot, preferred_element_type=jnp.float32)
    slot_index = jnp.sum(jnp.where(matches, earlier, 0.0), axis=1).astype(jnp.int32)
    sent_counts = jnp.sum(matches.astype(jnp.int32), axis=0)
    position = target * CAP + slot_index
    outgoing = jnp.zeros((slot_count, features), jnp.bfloat16).at[position].set(scaled)
    outgoing = outgoing.reshape(grp_count, wide_count, CAP, features)
    sent_counts = sent_counts.reshape(grp_count, wide_count, 1)

    def there(value):
        value = lax.all_to_all(value, GRP, split_axis=0, concat_axis=0, tiled=True)
        return lax.all_to_all(value, "wide", split_axis=1, concat_axis=1, tiled=True)

    arrived = there(outgoing).reshape(slot_count, features)
    counts_each = jnp.repeat(there(sent_counts).reshape(workers), CAP)
    slot_ids = jnp.arange(slot_count, dtype=jnp.int32)
    filled = slot_ids % CAP < counts_each
    paired = filled[:, None] & filled[None, :] & (slot_ids[:, None] != slot_ids[None, :])
    scores = lax.dot_general(
        arrived, arrived, (((1,), (1,)), ((), ())), preferred_element_type=jnp.float32
    )
    highest = jnp.max(jnp.where(paired, scores, -1e30), axis=1)
    back = highest.reshape(grp_count, wide_count, CAP)
    back = lax.all_to_all(back, "wide", split_axis=1, concat_axis=1, tiled=True)
    back = lax.all_to_all(back, GRP, split_axis=0, concat_axis=0, tiled=True)
    own_best = back.reshape(slot_count)[position]
    return jnp.where(own_best > -1e29, own_best, 0.0)


def z_shift(step):
    return [(z, (z + step) % PLANES) for z in range(PLANES)]


def after(value, *others):
    return lax.optimization_barrier((value,) + others)[0]


def call(kernel, out_shape, flops, **settings):
    return pl.pallas_call(
        kernel,
        out_shape=out_shape,
        compiler_params=pltpu.CompilerParams(vmem_limit_bytes=VMEM_LIMIT),
        cost_estimate=pl.CostEstimate(
            flops=flops, bytes_accessed=8 * 2**20, transcendentals=0
        ),
        **settings,
    )


def whole(value):
    return pl.BlockSpec(value.shape, lambda *_: (0,) * value.ndim)


def columns(rows, tile, first=0):
    return pl.BlockSpec((rows, tile), lambda i: (0, first + i))


def vmem():
    return pl.BlockSpec(memory_space=pltpu.VMEM)


def smem():
    return pl.BlockSpec(memory_space=pltpu.SMEM)


def iota(shape, axis):
    return lax.broadcasted_iota(jnp.int32, shape, axis)


def select_rows(pick, rows):
    return jnp.dot(pick, rows, preferred_element_type=jnp.float32)


def plan_kernel(
    where_ref,
    target_ref,
    x_ref,
    list_ref,
    wide_ref,
    fill_ref,
    note_ref,
    scale_ref,
    back_ref,
    flag_ref,
    squares,
):
    step = pl.program_id(0)
    f32, bf16 = jnp.float32, jnp.bfloat16
    part = jnp.zeros((HALF, 128), f32)
    for first in range(0, x_ref.shape[1], 128):
        values = x_ref[:, first : first + 128].astype(f32)
        part = part + values * values

    @pl.when(step == 0)
    def _():
        squares[...] = part
        z = where_ref[0]
        target = target_ref[...]
        across = (target == iota((WORKERS, HALF), 0)).astype(bf16)
        earlier = (iota((HALF, HALF), 0) < iota((HALF, HALF), 1)).astype(bf16)
        before = select_rows(across, earlier)
        counts = lax.dot_general(
            jnp.ones((16, HALF), bf16),
            across,
            (((1,), (1,)), ((), ())),
            preferred_element_type=f32,
        )
        down, over = iota((WORKERS, WORKERS), 0), iota((WORKERS, WORKERS), 1)
        same = down // PER_PLANE == over // PER_PLANE
        ahead = select_rows(counts.astype(bf16), (same & (down < over)).astype(bf16))[0:1, :]
        counts = counts[0:1, :]
        across = across.astype(f32)
        counts_down = jnp.sum(across, axis=1, keepdims=True)
        ahead_down = select_rows(
            (same & (over < down)).astype(bf16),
            jnp.broadcast_to(counts_down, (WORKERS, 128)).astype(bf16),
        )[:, 0:1]
        rank = jnp.sum(across * before, axis=0, keepdims=True).astype(jnp.int32)
        place = jnp.sum(across * (before + ahead_down), axis=0, keepdims=True).astype(jnp.int32)
        distance = (target // PER_PLANE - z) & (PLANES - 1)
        cluster_distance = (iota((1, WORKERS), 1) // PER_PLANE - z) & (PLANES - 1)
        n = [
            jnp.sum(jnp.where(cluster_distance == d, counts, 0.0), axis=1, keepdims=True).astype(
                jnp.int32
            )
            for d in range(PLANES)
        ]
        low = functools.reduce(
            jnp.maximum,
            (
                jnp.zeros_like(n[4]),
                n[4] - CAPS[3] + 1,
                n[4] + n[5] - CAPS[2] + 1,
                n[4] + n[5] + n[6] - CAPS[1] + 1,
                n[4] + n[5] + n[6] + n[7] - CAPS[0] + 1,
            ),
        )
        high = functools.reduce(
            jnp.minimum,
            (
                n[4],
                jnp.full_like(n[4], CAPS[3] - 1),
                CAPS[2] - 1 - n[3],
                CAPS[1] - 1 - n[3] - n[2],
                CAPS[0] - 1 - n[3] - n[2] - n[1],
            ),
        )
        to_right = jnp.clip((low + high) >> 1, 0, n[4])
        starts = [
            None,
            to_right + n[3] + n[2],
            to_right + n[3],
            to_right,
            to_right,
            n[4] - to_right,
            n[4] - to_right + n[5],
            n[4] - to_right + n[5] + n[6],
        ]

        def by_distance(which):
            value = jnp.zeros(which.shape, jnp.int32)
            for d in range(1, PLANES):
                value = jnp.where(which == d, starts[d], value)
            return value

        start = by_distance(distance)
        far_right = (distance == 4) & (place < to_right)
        far_left = (distance == 4) & (place >= to_right)
        goes_right = ((distance >= 1) & (distance <= 3)) | far_right
        on_list = jnp.where(far_right, place, jnp.where(far_left, place - to_right, start + place))
        list_place = jnp.where(
            distance == 0,
            2 * LIST + place,
            jnp.where(
                on_list >= LIST - 1, -1, jnp.where(goes_right, 1 + on_list, LIST + 1 + on_list)
            ),
        )
        list_ref[...] = (iota((2 * LIST + OWN_LIST, HALF), 0) == list_place).astype(bf16)
        wide_place = (target // WIDE % 2) * HALF + target % WIDE * 32 + distance * CAP + rank
        wide_match = (iota((OUT, HALF), 0) == wide_place).astype(f32)
        wide_ref[...] = wide_match.astype(bf16)
        fill_ref[...] = MARK * (1.0 - jnp.sum(wide_match, axis=1, keepdims=True))
        note_ref[...] = jnp.zeros((1, NOTE), f32)
        note_ref[:, 0:WORKERS] = counts
        note_ref[:, WORKERS : 2 * WORKERS] = ahead
        note_ref[:, 2 * WORKERS : 3 * WORKERS] = by_distance(cluster_distance).astype(f32)
        back_ref[...] = target * CAP + rank
        flag_ref[...] = jnp.broadcast_to((low > high).astype(f32), (1, 128))

    @pl.when(step > 0)
    def _():
        squares[...] += part

    @pl.when(step == pl.num_programs(0) - 1)
    def _():
        features = pl.num_programs(0) * x_ref.shape[1]
        spread = jnp.sum(squares[...], axis=1, keepdims=True) * (1.0 / features)
        scale_ref[...] = lax.rsqrt(spread + 1e-06) * features ** (-0.25)


def plan(where, targets, embeddings):
    f32, bf16 = jnp.float32, jnp.bfloat16
    shapes = [
        jax.ShapeDtypeStruct((2 * LIST + OWN_LIST, HALF), bf16),
        jax.ShapeDtypeStruct((OUT, HALF), bf16),
        jax.ShapeDtypeStruct((OUT, 1), f32),
        jax.ShapeDtypeStruct((1, NOTE), f32),
        jax.ShapeDtypeStruct((HALF, 1), f32),
        jax.ShapeDtypeStruct((1, HALF), jnp.int32),
        jax.ShapeDtypeStruct((1, 128), f32),
    ]
    return call(
        plan_kernel,
        shapes,
        10**9,
        grid=(4,),
        in_specs=[smem(), whole(targets), columns(HALF, embeddings.shape[1] // 4)],
        out_specs=[whole(shape) for shape in shapes],
        scratch_shapes=[pltpu.VMEM((HALF, 128), f32)],
    )(where, targets, embeddings)


def scaled_rows(x_ref, scale_ref):
    return (x_ref[...].astype(jnp.float32) * scale_ref[...]).astype(jnp.bfloat16)


def pack_lists_kernel(pick_ref, note_ref, scale_ref, x_ref, right_ref, left_ref, own_ref):
    packed = select_rows(pick_ref[...], scaled_rows(x_ref, scale_ref))
    first = iota((LIST, 1), 0) == 0
    note = note_ref[...]
    right_ref[...] = jnp.where(first, note, packed[0:LIST, :]).astype(jnp.bfloat16)
    left_ref[...] = jnp.where(first, note, packed[LIST : 2 * LIST, :]).astype(jnp.bfloat16)
    own_ref[...] = packed[2 * LIST :, :].astype(jnp.bfloat16)


def pack_lists(pick, note, scale, embeddings, first_column, width):
    tile = 256
    parts = (LIST, LIST, OWN_LIST)
    return call(
        pack_lists_kernel,
        [jax.ShapeDtypeStruct((rows, width), jnp.bfloat16) for rows in parts],
        2 * pick.shape[0] * HALF * width,
        grid=(width // tile,),
        in_specs=[
            whole(pick),
            columns(1, tile),
            whole(scale),
            columns(HALF, tile, first_column // tile),
        ],
        out_specs=[columns(rows, tile) for rows in parts],
    )(pick, note, scale, embeddings)


def pack_wide_kernel(pick_ref, fill_ref, scale_ref, x_ref, out_ref):
    packed = select_rows(pick_ref[...], scaled_rows(x_ref, scale_ref))
    out_ref[...] = (packed + fill_ref[...]).astype(jnp.bfloat16)


def pack_wide(pick, fill, scale, embeddings, first_column, width):
    tile = 256
    return call(
        pack_wide_kernel,
        jax.ShapeDtypeStruct((OUT, width), jnp.bfloat16),
        2 * OUT * HALF * width,
        grid=(width // tile,),
        in_specs=[
            whole(pick),
            whole(fill),
            whole(scale),
            columns(HALF, tile, first_column // tile),
        ],
        out_specs=columns(OUT, tile),
    )(pick, fill, scale, embeddings)


def reorder_kernel(pick_ref, x_ref, *out_refs):
    moved = select_rows(pick_ref[...], x_ref[...]).astype(jnp.bfloat16)
    for index, out_ref in enumerate(out_refs):
        out_ref[...] = moved[index * 128 : index * 128 + 128, :]


def reorder(pick, value):
    width = value.shape[1]
    tile = 256
    return call(
        reorder_kernel,
        [jax.ShapeDtypeStruct((128, width), jnp.bfloat16)] * PLANES,
        2 * OUT * OUT * width,
        grid=(width // tile,),
        in_specs=[whole(pick), columns(OUT, tile)],
        out_specs=[columns(128, tile)] * PLANES,
    )(pick, value)


def slots_kernel(where_ref, note_ref, *refs):
    firsts, out_ref, told = refs[:-2], refs[-2], refs[-1]
    told[...] = jnp.zeros(told.shape, jnp.float32)
    told[0:1, :] = note_ref[...]
    for index, first in enumerate(firsts):
        told[index + 1 : index + 2, :] = first[...].astype(jnp.float32)[0:1, :]
    slot = iota((OUT, 1), 0)
    step, rank = slot // CAP % PLANES, slot % CAP
    by_step = (iota((OUT, 16), 1) == step).astype(jnp.bfloat16)
    mine = iota((OUT, WORKERS), 1) == where_ref[0] * PER_PLANE + slot // 32

    def heard(index):
        told_here = told[:, index * WORKERS : index * WORKERS + WORKERS].astype(jnp.bfloat16)
        value = jnp.where(mine, select_rows(by_step, told_here), 0.0)
        return jnp.sum(value, axis=1, keepdims=True).astype(jnp.int32)

    count, place, start = heard(0), heard(1) + rank, heard(2)
    offsets = [OWN_LIST]
    for cap in CAPS + CAPS:
        offsets.append(offsets[-1] + cap)
    found = jnp.where(
        place < start, offsets[3] + 1 + place, offsets[7] + 1 + place - start
    )
    for d, block in ((1, 0), (2, 1), (3, 2), (5, 6), (6, 5), (7, 4)):
        found = jnp.where(step == d, offsets[block] + 1 + start + place, found)
    found = jnp.where(step == 0, place, found)
    found = jnp.where(rank < count, found, -1)
    out_ref[...] = (found == iota(out_ref.shape, 1)).astype(jnp.bfloat16)


def slots(where, note, blocks):
    firsts = [blocks[b] for b in (0, 1, 2, 3, 6, 5, 4)]
    shape = jax.ShapeDtypeStruct((OUT, OWN_LIST + 2 * sum(CAPS)), jnp.bfloat16)
    return call(
        slots_kernel,
        shape,
        10**9,
        grid=(1,),
        in_specs=[smem(), whole(note)]
        + [pl.BlockSpec((16, NOTE), lambda i: (0, 0)) for _ in firsts],
        out_specs=whole(shape),
        scratch_shapes=[pltpu.VMEM((16, NOTE), jnp.float32)],
    )(where, note, *firsts)


def repack_kernel(turn, pick_ref, *refs):
    blocks, out_ref, held = refs[:-2], refs[-2], refs[-1]
    for chunk in range(2):

        @pl.when((pl.program_id(0) >= turn) == bool(chunk))
        def _(chunk=chunk):
            base = 0
            for block in blocks[chunk * 9 : chunk * 9 + 9]:
                rows = block.shape[0]
                held[base : base + rows, :] = block[...]
                base += rows

    out_ref[...] = select_rows(pick_ref[...], held[...]).astype(jnp.bfloat16)


def repack(pick, first_blocks, second_blocks):
    tile = 256
    depth = pick.shape[1]
    turn = first_blocks[0].shape[1] // tile
    steps = turn + second_blocks[0].shape[1] // tile
    in_specs = [whole(pick)]
    for block in first_blocks:
        in_specs.append(
            pl.BlockSpec((block.shape[0], tile), lambda i: (0, jnp.minimum(i, turn - 1)))
        )
    for block in second_blocks:
        in_specs.append(
            pl.BlockSpec((block.shape[0], tile), lambda i: (0, jnp.maximum(i - turn, 0)))
        )
    return call(
        functools.partial(repack_kernel, turn),
        jax.ShapeDtypeStruct((OUT, steps * tile), jnp.bfloat16),
        2 * OUT * depth * steps * tile,
        grid=(steps,),
        in_specs=in_specs,
        out_specs=columns(OUT, tile),
        scratch_shapes=[pltpu.VMEM((depth, tile), jnp.bfloat16)],
    )(pick, *first_blocks, *second_blocks)


def gram_kernel(pick_ref, x_ref, out_ref, held):
    step = pl.program_id(0)
    held[step] = select_rows(pick_ref[...], x_ref[...]).astype(jnp.bfloat16)

    @pl.when(step == pl.num_programs(0) - 1)
    def _():
        for tile in range(0, OUT, ROW_TILE):
            part = 0.0
            for index in range(held.shape[0]):
                part = part + lax.dot_general(
                    held[index, tile : tile + ROW_TILE, :],
                    held[index],
                    (((1,), (1,)), ((), ())),
                    preferred_element_type=jnp.float32,
                )
            out_ref[tile : tile + ROW_TILE, :] = part


def gram(pick, value):
    width = value.shape[1]
    tile = 768
    return call(
        gram_kernel,
        jax.ShapeDtypeStruct((OUT, OUT), jnp.float32),
        4 * OUT * OUT * width,
        grid=(width // tile,),
        in_specs=[whole(pick), columns(OUT, tile)],
        out_specs=pl.BlockSpec((OUT, OUT), lambda i: (0, 0)),
        scratch_shapes=[pltpu.VMEM((width // tile, OUT, tile), jnp.bfloat16)],
    )(pick, value)


def best_kernel(where_ref, flag_ref, total_ref, *refs):
    blocks, out_ref, held, scores = refs[:PLANES], refs[PLANES], refs[-2], refs[-1]
    for index, block in enumerate(blocks):
        held[index * 128 : index * 128 + 128, :] = block[...]
    best = jnp.full((1, OUT), -1e30, jnp.float32)
    for tile in range(0, OUT, ROW_TILE):
        part = total_ref[tile : tile + ROW_TILE, :] + lax.dot_general(
            held[tile : tile + ROW_TILE, :],
            held[...],
            (((1,), (1,)), ((), ())),
            preferred_element_type=jnp.float32,
        )
        same = tile + iota((ROW_TILE, OUT), 0) == iota((ROW_TILE, OUT), 1)
        squares = jnp.sum(jnp.where(same, part, 0.0), axis=1, keepdims=True)
        closed = same | (squares >= REAL_MAX)
        best = jnp.maximum(
            best, jnp.max(jnp.where(closed, -1e30, part), axis=0, keepdims=True)
        )
    best = jnp.where(best > -1e29, best, 0.0)
    best = jnp.where(flag_ref[0:1, 0:1] > 0.5, 1e30, best)
    for d in range(PLANES):
        plane = (where_ref[0] - d) & (PLANES - 1)
        out_ref[pl.ds(pl.multiple_of(plane * 32, 32), 32), :] = jnp.broadcast_to(
            best[:, d * 128 : d * 128 + 128], (32, 128)
        )


def best_of(where, flag, total, blocks):
    width = blocks[0].shape[1]
    return call(
        best_kernel,
        jax.ShapeDtypeStruct((WORKERS, 128), jnp.float32),
        2 * OUT * OUT * width,
        in_specs=[smem()] + [vmem()] * (2 + PLANES),
        out_specs=vmem(),
        scratch_shapes=[
            pltpu.VMEM((OUT, width), jnp.bfloat16),
            pltpu.VMEM((8, 128), jnp.float32),
        ],
    )(where, flag, total, *blocks)


def on_device(embeddings, worker_of_row):
    i32 = jnp.int32
    core = lax.axis_index("core")
    wide = lax.axis_index("wide")
    where = lax.axis_index("z").astype(i32).reshape(1)
    list_pick, wide_pick, wide_fill, note, scale, back_place, flag = plan(
        where, worker_of_row.reshape(1, HALF), embeddings
    )

    packed, own = [], []
    for f in range(2):
        right, left, mine = pack_lists(
            list_pick, note, scale, embeddings, sum(Z_FIRST[:f]), Z_FIRST[f]
        )
        packed.append((right, left))
        own.append(mine)

    wide_rows = pack_wide(after(wide_pick, packed[0][0]), wide_fill, scale, embeddings, sum(Z_FIRST), WIDE_FIRST)
    wide_back = lax.all_to_all(wide_rows, CORE_WIDE, 0, 0, tiled=True)

    slot_ids = jnp.arange(OUT, dtype=i32)
    final = slot_ids[:, None]
    step_of, core_of, column_of = final // 128, final // 64 % 2, final // 4 % WIDE
    final_from = core_of * HALF + column_of * 32 + step_of * CAP + final % CAP
    final_order = (final_from == slot_ids[None, :]).astype(jnp.bfloat16)

    got = [([], []), ([], [])]
    for hop in range(4):
        if hop == 3:
            blocks = reorder(after(final_order, got[0][0][2]), wide_back)
        for f in range(2):
            for side, steps in enumerate((z_shift(1), z_shift(-1))):
                if hop == 0:
                    block = packed[f][side]
                else:
                    block = got[f][side][-1][: CAPS[hop]]
                if hop == 1:
                    block = after(block, wide_rows)
                if hop == 3 and f == 1:
                    block = after(block, blocks[1])
                got[f][side].append(lax.ppermute(block, "z", steps))
    got = [rights + lefts for rights, lefts in got]
    last = [blocks[0]] + [None] * 7
    for steps, gate in (((1, 7), ()), ((2, 6), (1, 7)), ((3, 5, 4), (2, 6))):
        for step in steps:
            block = blocks[step]
            if gate:
                block = after(block, *[last[done] for done in gate])
            last[step] = lax.ppermute(block, "z", z_shift(step))

    slot_pick = slots(where, note, got[0])
    packed = repack(slot_pick, [own[0]] + got[0], [own[1]] + got[1])
    packed = after(packed, wide_back, last[1], last[7])
    arrived = lax.all_to_all(packed, CORE_WIDE, 0, 0, tiled=True)
    best = best_of(where, flag, gram(final_order, arrived), last)

    back = lax.all_to_all(best, ALL, 0, 0, tiled=True)
    failed = jnp.max(back) > 1e29
    mine = lax.dynamic_slice(back, (0, core * 64 + wide * CAP), (WORKERS, CAP))
    result = jnp.sum(
        jnp.where(back_place == slot_ids[:, None], mine.reshape(OUT)[:, None], 0.0), axis=0
    )
    return lax.cond(failed, padded_plan, lambda *_: result, embeddings, worker_of_row)


def solution(mesh):
    split = jax.sharding.Mesh(mesh.devices.reshape(PLANES, 2, WIDE), ALL)
    placed = (P(ALL, None), P(ALL, None))
    return jax.shard_map(
        on_device, mesh=split, in_specs=placed, out_specs=P(ALL), check_vma=False
    )
```

```python
import functools

import jax
import jax.numpy as jnp
from jax import lax
from jax.experimental import pallas as pl
from jax.experimental.pallas import tpu as pltpu
from jax.sharding import PartitionSpec as P

GRP = ("z", "core")
CORE_WIDE = ("core", "wide")
ALL = ("z", "core", "wide")
PLANES = 8
WIDE = 16
PER_PLANE = 32
WORKERS = 256
CAP = 4
HALF = 512
OUT = 1024
CAPS = (256, 192, 128, 64)
LIST = CAPS[0]
OWN_LIST = 128
Z_FIRST = (1280, 1024)
WIDE_FIRST = 1792
MARK = 2.0
REAL_MAX = 100.0
ROW_TILE = 256
NOTE = 1280
VMEM_LIMIT = 56 * 2**20


def padded_plan(embeddings, worker_of_row):
    row_count, features = embeddings.shape
    grp_count = lax.axis_size("z") * lax.axis_size("core")
    wide_count = lax.axis_size("wide")
    workers = grp_count * wide_count
    slot_count = workers * CAP
    values = embeddings.astype(jnp.float32)
    spread = jnp.mean(values * values, axis=1, keepdims=True)
    scaled = (values * lax.rsqrt(spread + 1e-06) * features ** (-0.25)).astype(jnp.bfloat16)
    target = worker_of_row[:, 0]
    matches = target[:, None] == jnp.arange(workers, dtype=jnp.int32)[None, :]
    one_hot = matches.astype(jnp.bfloat16)
    row_ids = jnp.arange(row_count, dtype=jnp.int32)
    earlier_mask = (row_ids[:, None] > row_ids[None, :]).astype(jnp.bfloat16)
    earlier = jnp.dot(earlier_mask, one_hot, preferred_element_type=jnp.float32)
    slot_index = jnp.sum(jnp.where(matches, earlier, 0.0), axis=1).astype(jnp.int32)
    sent_counts = jnp.sum(matches.astype(jnp.int32), axis=0)
    position = target * CAP + slot_index
    outgoing = jnp.zeros((slot_count, features), jnp.bfloat16).at[position].set(scaled)
    outgoing = outgoing.reshape(grp_count, wide_count, CAP, features)
    sent_counts = sent_counts.reshape(grp_count, wide_count, 1)

    def there(value):
        value = lax.all_to_all(value, GRP, split_axis=0, concat_axis=0, tiled=True)
        return lax.all_to_all(value, "wide", split_axis=1, concat_axis=1, tiled=True)

    arrived = there(outgoing).reshape(slot_count, features)
    counts_each = jnp.repeat(there(sent_counts).reshape(workers), CAP)
    slot_ids = jnp.arange(slot_count, dtype=jnp.int32)
    filled = slot_ids % CAP < counts_each
    paired = filled[:, None] & filled[None, :] & (slot_ids[:, None] != slot_ids[None, :])
    scores = lax.dot_general(
        arrived, arrived, (((1,), (1,)), ((), ())), preferred_element_type=jnp.float32
    )
    highest = jnp.max(jnp.where(paired, scores, -1e30), axis=1)
    back = highest.reshape(grp_count, wide_count, CAP)
    back = lax.all_to_all(back, "wide", split_axis=1, concat_axis=1, tiled=True)
    back = lax.all_to_all(back, GRP, split_axis=0, concat_axis=0, tiled=True)
    own_best = back.reshape(slot_count)[position]
    return jnp.where(own_best > -1e29, own_best, 0.0)


def z_shift(step):
    return [(z, (z + step) % PLANES) for z in range(PLANES)]


def after(value, *others):
    return lax.optimization_barrier((value,) + others)[0]


def call(kernel, out_shape, flops, **settings):
    return pl.pallas_call(
        kernel,
        out_shape=out_shape,
        compiler_params=pltpu.CompilerParams(vmem_limit_bytes=VMEM_LIMIT),
        cost_estimate=pl.CostEstimate(
            flops=flops, bytes_accessed=8 * 2**20, transcendentals=0
        ),
        **settings,
    )


def whole(value):
    return pl.BlockSpec(value.shape, lambda *_: (0,) * value.ndim)


def columns(rows, tile, first=0):
    return pl.BlockSpec((rows, tile), lambda i: (0, first + i))


def window(rows, tile, first):
    return pl.BlockSpec((pl.Element(rows), pl.Element(tile)), lambda i: (0, pl.multiple_of(first + i * tile, 128)))


def vmem():
    return pl.BlockSpec(memory_space=pltpu.VMEM)


def smem():
    return pl.BlockSpec(memory_space=pltpu.SMEM)


def iota(shape, axis):
    return lax.broadcasted_iota(jnp.int32, shape, axis)


def select_rows(pick, rows):
    return jnp.dot(pick, rows, preferred_element_type=jnp.float32)


def plan_kernel(
    where_ref,
    target_ref,
    x_ref,
    list_ref,
    wide_ref,
    fill_ref,
    note_ref,
    scale_ref,
    back_ref,
    flag_ref,
    squares,
):
    step = pl.program_id(0)
    f32, bf16 = jnp.float32, jnp.bfloat16
    part = jnp.zeros((HALF, 128), f32)
    for first in range(0, x_ref.shape[1], 128):
        values = x_ref[:, first : first + 128].astype(f32)
        part = part + values * values

    @pl.when(step == 0)
    def _():
        squares[...] = part
        z = where_ref[0]
        target = target_ref[...]
        across = (target == iota((WORKERS, HALF), 0)).astype(bf16)
        earlier = (iota((HALF, HALF), 0) < iota((HALF, HALF), 1)).astype(bf16)
        before = select_rows(across, earlier)
        counts = lax.dot_general(
            jnp.ones((16, HALF), bf16),
            across,
            (((1,), (1,)), ((), ())),
            preferred_element_type=f32,
        )
        down, over = iota((WORKERS, WORKERS), 0), iota((WORKERS, WORKERS), 1)
        same = down // PER_PLANE == over // PER_PLANE
        ahead = select_rows(counts.astype(bf16), (same & (down < over)).astype(bf16))[0:1, :]
        counts = counts[0:1, :]
        across = across.astype(f32)
        counts_down = jnp.sum(across, axis=1, keepdims=True)
        ahead_down = select_rows(
            (same & (over < down)).astype(bf16),
            jnp.broadcast_to(counts_down, (WORKERS, 128)).astype(bf16),
        )[:, 0:1]
        rank = jnp.sum(across * before, axis=0, keepdims=True).astype(jnp.int32)
        place = jnp.sum(across * (before + ahead_down), axis=0, keepdims=True).astype(jnp.int32)
        distance = (target // PER_PLANE - z) & (PLANES - 1)
        cluster_distance = (iota((1, WORKERS), 1) // PER_PLANE - z) & (PLANES - 1)
        n = [
            jnp.sum(jnp.where(cluster_distance == d, counts, 0.0), axis=1, keepdims=True).astype(
                jnp.int32
            )
            for d in range(PLANES)
        ]
        low = functools.reduce(
            jnp.maximum,
            (
                jnp.zeros_like(n[4]),
                n[4] - CAPS[3] + 1,
                n[4] + n[5] - CAPS[2] + 1,
                n[4] + n[5] + n[6] - CAPS[1] + 1,
                n[4] + n[5] + n[6] + n[7] - CAPS[0] + 1,
            ),
        )
        high = functools.reduce(
            jnp.minimum,
            (
                n[4],
                jnp.full_like(n[4], CAPS[3] - 1),
                CAPS[2] - 1 - n[3],
                CAPS[1] - 1 - n[3] - n[2],
                CAPS[0] - 1 - n[3] - n[2] - n[1],
            ),
        )
        to_right = jnp.clip((low + high) >> 1, 0, n[4])
        starts = [
            None,
            to_right + n[3] + n[2],
            to_right + n[3],
            to_right,
            to_right,
            n[4] - to_right,
            n[4] - to_right + n[5],
            n[4] - to_right + n[5] + n[6],
        ]

        def by_distance(which):
            value = jnp.zeros(which.shape, jnp.int32)
            for d in range(1, PLANES):
                value = jnp.where(which == d, starts[d], value)
            return value

        start = by_distance(distance)
        far_right = (distance == 4) & (place < to_right)
        far_left = (distance == 4) & (place >= to_right)
        goes_right = ((distance >= 1) & (distance <= 3)) | far_right
        on_list = jnp.where(far_right, place, jnp.where(far_left, place - to_right, start + place))
        list_place = jnp.where(
            distance == 0,
            2 * LIST + place,
            jnp.where(
                on_list >= LIST - 1, -1, jnp.where(goes_right, 1 + on_list, LIST + 1 + on_list)
            ),
        )
        list_ref[...] = (iota((2 * LIST + OWN_LIST, HALF), 0) == list_place).astype(bf16)
        wide_place = (target // WIDE % 2) * HALF + target % WIDE * 32 + distance * CAP + rank
        wide_match = (iota((OUT, HALF), 0) == wide_place).astype(f32)
        wide_ref[...] = wide_match.astype(bf16)
        fill_ref[...] = MARK * (1.0 - jnp.sum(wide_match, axis=1, keepdims=True))
        note_ref[...] = jnp.zeros((1, NOTE), f32)
        note_ref[:, 0:WORKERS] = counts
        note_ref[:, WORKERS : 2 * WORKERS] = ahead
        note_ref[:, 2 * WORKERS : 3 * WORKERS] = by_distance(cluster_distance).astype(f32)
        back_ref[...] = target * CAP + rank
        flag_ref[...] = jnp.broadcast_to((low > high).astype(f32), (1, 128))

    @pl.when(step > 0)
    def _():
        squares[...] += part

    @pl.when(step == pl.num_programs(0) - 1)
    def _():
        features = pl.num_programs(0) * x_ref.shape[1]
        spread = jnp.sum(squares[...], axis=1, keepdims=True) * (1.0 / features)
        scale_ref[...] = lax.rsqrt(spread + 1e-06) * features ** (-0.25)


def plan(where, targets, embeddings):
    f32, bf16 = jnp.float32, jnp.bfloat16
    shapes = [
        jax.ShapeDtypeStruct((2 * LIST + OWN_LIST, HALF), bf16),
        jax.ShapeDtypeStruct((OUT, HALF), bf16),
        jax.ShapeDtypeStruct((OUT, 1), f32),
        jax.ShapeDtypeStruct((1, NOTE), f32),
        jax.ShapeDtypeStruct((HALF, 1), f32),
        jax.ShapeDtypeStruct((1, HALF), jnp.int32),
        jax.ShapeDtypeStruct((1, 128), f32),
    ]
    return call(
        plan_kernel,
        shapes,
        10**9,
        grid=(4,),
        in_specs=[smem(), whole(targets), columns(HALF, embeddings.shape[1] // 4)],
        out_specs=[whole(shape) for shape in shapes],
        scratch_shapes=[pltpu.VMEM((HALF, 128), f32)],
    )(where, targets, embeddings)


def scaled_rows(x_ref, scale_ref):
    return (x_ref[...].astype(jnp.float32) * scale_ref[...]).astype(jnp.bfloat16)


def pack_lists_kernel(pick_ref, note_ref, scale_ref, x_ref, right_ref, left_ref, own_ref):
    packed = select_rows(pick_ref[...], scaled_rows(x_ref, scale_ref))
    first = iota((LIST, 1), 0) == 0
    note = note_ref[...]
    right_ref[...] = jnp.where(first, note, packed[0:LIST, :]).astype(jnp.bfloat16)
    left_ref[...] = jnp.where(first, note, packed[LIST : 2 * LIST, :]).astype(jnp.bfloat16)
    own_ref[...] = packed[2 * LIST :, :].astype(jnp.bfloat16)


def pack_lists(pick, note, scale, embeddings, first_column, width):
    tile = width // 2
    parts = (LIST, LIST, OWN_LIST)
    return call(
        pack_lists_kernel,
        [jax.ShapeDtypeStruct((rows, width), jnp.bfloat16) for rows in parts],
        2 * pick.shape[0] * HALF * width,
        grid=(width // tile,),
        in_specs=[
            whole(pick),
            columns(1, tile),
            whole(scale),
            window(HALF, tile, first_column),
        ],
        out_specs=[columns(rows, tile) for rows in parts],
    )(pick, note, scale, embeddings)


def pack_wide_kernel(pick_ref, fill_ref, scale_ref, x_ref, out_ref):
    packed = select_rows(pick_ref[...], scaled_rows(x_ref, scale_ref))
    out_ref[...] = (packed + fill_ref[...]).astype(jnp.bfloat16)


def pack_wide(pick, fill, scale, embeddings, first_column, width):
    tile = width // 2
    return call(
        pack_wide_kernel,
        jax.ShapeDtypeStruct((OUT, width), jnp.bfloat16),
        2 * OUT * HALF * width,
        grid=(width // tile,),
        in_specs=[
            whole(pick),
            whole(fill),
            whole(scale),
            window(HALF, tile, first_column),
        ],
        out_specs=columns(OUT, tile),
    )(pick, fill, scale, embeddings)


def reorder_kernel(pick_ref, x_ref, *out_refs):
    moved = select_rows(pick_ref[...], x_ref[...]).astype(jnp.bfloat16)
    for index, out_ref in enumerate(out_refs):
        out_ref[...] = moved[index * 128 : index * 128 + 128, :]


def reorder(pick, value):
    width = value.shape[1]
    tile = 256
    return call(
        reorder_kernel,
        [jax.ShapeDtypeStruct((128, width), jnp.bfloat16)] * PLANES,
        2 * OUT * OUT * width,
        grid=(width // tile,),
        in_specs=[whole(pick), columns(OUT, tile)],
        out_specs=[columns(128, tile)] * PLANES,
    )(pick, value)


def slots_kernel(where_ref, note_ref, *refs):
    firsts, out_ref, told = refs[:-2], refs[-2], refs[-1]
    told[...] = jnp.zeros(told.shape, jnp.float32)
    told[0:1, :] = note_ref[...]
    for index, first in enumerate(firsts):
        told[index + 1 : index + 2, :] = first[...].astype(jnp.float32)[0:1, :]
    slot = iota((OUT, 1), 0)
    step, rank = slot // CAP % PLANES, slot % CAP
    by_step = (iota((OUT, 16), 1) == step).astype(jnp.bfloat16)
    mine = iota((OUT, WORKERS), 1) == where_ref[0] * PER_PLANE + slot // 32

    def heard(index):
        told_here = told[:, index * WORKERS : index * WORKERS + WORKERS].astype(jnp.bfloat16)
        value = jnp.where(mine, select_rows(by_step, told_here), 0.0)
        return jnp.sum(value, axis=1, keepdims=True).astype(jnp.int32)

    count, place, start = heard(0), heard(1) + rank, heard(2)
    offsets = [OWN_LIST]
    for cap in CAPS + CAPS:
        offsets.append(offsets[-1] + cap)
    found = jnp.where(
        place < start, offsets[3] + 1 + place, offsets[7] + 1 + place - start
    )
    for d, block in ((1, 0), (2, 1), (3, 2), (5, 6), (6, 5), (7, 4)):
        found = jnp.where(step == d, offsets[block] + 1 + start + place, found)
    found = jnp.where(step == 0, place, found)
    found = jnp.where(rank < count, found, -1)
    out_ref[...] = (found == iota(out_ref.shape, 1)).astype(jnp.bfloat16)


def slots(where, note, blocks):
    firsts = [blocks[b] for b in (0, 1, 2, 3, 6, 5, 4)]
    shape = jax.ShapeDtypeStruct((OUT, OWN_LIST + 2 * sum(CAPS)), jnp.bfloat16)
    return call(
        slots_kernel,
        shape,
        10**9,
        grid=(1,),
        in_specs=[smem(), whole(note)]
        + [pl.BlockSpec((16, NOTE), lambda i: (0, 0)) for _ in firsts],
        out_specs=whole(shape),
        scratch_shapes=[pltpu.VMEM((16, NOTE), jnp.float32)],
    )(where, note, *firsts)


def repack_kernel(turn, pick_ref, *refs):
    blocks, out_ref, held = refs[:-2], refs[-2], refs[-1]
    step = pl.program_id(0)
    for chunk in range(2):

        @pl.when((step >= turn) == bool(chunk))
        def _(chunk=chunk):
            first = pl.multiple_of((step - chunk * turn) * 256, 256)
            base = 0
            for block in blocks[chunk * 9 : chunk * 9 + 9]:
                rows = block.shape[0]
                held[base : base + rows, :] = block[:, pl.ds(first, 256)]
                base += rows

    out_ref[...] = select_rows(pick_ref[...], held[...]).astype(jnp.bfloat16)


def repack(pick, first_blocks, second_blocks):
    tile = 256
    depth = pick.shape[1]
    turn = first_blocks[0].shape[1] // tile
    steps = turn + second_blocks[0].shape[1] // tile
    blocks = list(first_blocks) + list(second_blocks)
    return call(
        functools.partial(repack_kernel, turn),
        jax.ShapeDtypeStruct((OUT, steps * tile), jnp.bfloat16),
        2 * OUT * depth * steps * tile,
        grid=(steps,),
        in_specs=[whole(value) for value in [pick] + blocks],
        out_specs=columns(OUT, tile),
        scratch_shapes=[pltpu.VMEM((depth, tile), jnp.bfloat16)],
    )(pick, *blocks)


def gram_kernel(pick_ref, x_ref, out_ref, held):
    step = pl.program_id(0)
    held[step] = select_rows(pick_ref[...], x_ref[...]).astype(jnp.bfloat16)

    @pl.when(step == pl.num_programs(0) - 1)
    def _():
        for tile in range(0, OUT, ROW_TILE):
            part = 0.0
            for index in range(held.shape[0]):
                part = part + lax.dot_general(
                    held[index, tile : tile + ROW_TILE, :],
                    held[index],
                    (((1,), (1,)), ((), ())),
                    preferred_element_type=jnp.float32,
                )
            out_ref[tile : tile + ROW_TILE, :] = part


def gram(pick, value):
    width = value.shape[1]
    tile = 768
    return call(
        gram_kernel,
        jax.ShapeDtypeStruct((OUT, OUT), jnp.float32),
        4 * OUT * OUT * width,
        grid=(width // tile,),
        in_specs=[whole(pick), columns(OUT, tile)],
        out_specs=pl.BlockSpec((OUT, OUT), lambda i: (0, 0)),
        scratch_shapes=[pltpu.VMEM((width // tile, OUT, tile), jnp.bfloat16)],
    )(pick, value)


def best_kernel(where_ref, flag_ref, total_ref, *refs):
    blocks, out_ref, held, best_ref = refs[:PLANES], refs[PLANES], refs[-2], refs[-1]
    step = pl.program_id(0)

    @pl.when(step == 0)
    def _():
        for index, block in enumerate(blocks):
            held[index * 128 : index * 128 + 128, :] = block[...]
        best_ref[...] = jnp.full((1, OUT), -1e30, jnp.float32)

    first = pl.multiple_of(step * ROW_TILE, ROW_TILE)
    part = total_ref[...] + lax.dot_general(
        held[pl.ds(first, ROW_TILE), :],
        held[...],
        (((1,), (1,)), ((), ())),
        preferred_element_type=jnp.float32,
    )
    same = first + iota((ROW_TILE, OUT), 0) == iota((ROW_TILE, OUT), 1)
    squares = jnp.sum(jnp.where(same, part, 0.0), axis=1, keepdims=True)
    closed = same | (squares >= REAL_MAX)
    best = jnp.maximum(
        best_ref[...], jnp.max(jnp.where(closed, -1e30, part), axis=0, keepdims=True)
    )
    best_ref[...] = best

    @pl.when(step == pl.num_programs(0) - 1)
    def _():
        result = jnp.where(best > -1e29, best, 0.0)
        result = jnp.where(flag_ref[0:1, 0:1] > 0.5, 1e30, result)
        for d in range(PLANES):
            plane = (where_ref[0] - d) & (PLANES - 1)
            out_ref[pl.ds(pl.multiple_of(plane * 32, 32), 32), :] = jnp.broadcast_to(
                result[:, d * 128 : d * 128 + 128], (32, 128)
            )


def best_of(where, flag, total, blocks):
    width = blocks[0].shape[1]
    shape = jax.ShapeDtypeStruct((WORKERS, 128), jnp.float32)
    return call(
        best_kernel,
        shape,
        2 * OUT * OUT * width,
        grid=(OUT // ROW_TILE,),
        in_specs=[smem(), whole(flag), pl.BlockSpec((ROW_TILE, OUT), lambda i: (i, 0))]
        + [whole(block) for block in blocks],
        out_specs=whole(shape),
        scratch_shapes=[
            pltpu.VMEM((OUT, width), jnp.bfloat16),
            pltpu.VMEM((1, OUT), jnp.float32),
        ],
    )(where, flag, total, *blocks)


def on_device(embeddings, worker_of_row):
    i32 = jnp.int32
    core = lax.axis_index("core")
    wide = lax.axis_index("wide")
    where = lax.axis_index("z").astype(i32).reshape(1)
    list_pick, wide_pick, wide_fill, note, scale, back_place, flag = plan(
        where, worker_of_row.reshape(1, HALF), embeddings
    )

    packed, own = [], []
    for f in range(2):
        right, left, mine = pack_lists(
            list_pick, note, scale, embeddings, sum(Z_FIRST[:f]), Z_FIRST[f]
        )
        packed.append((right, left))
        own.append(mine)

    wide_rows = pack_wide(
        after(wide_pick, packed[0][0]), wide_fill, scale, embeddings, sum(Z_FIRST), WIDE_FIRST
    )
    wide_back = lax.all_to_all(wide_rows, CORE_WIDE, 0, 0, tiled=True)

    slot_ids = jnp.arange(OUT, dtype=i32)
    final = slot_ids[:, None]
    step_of, core_of, column_of = final // 128, final // 64 % 2, final // 4 % WIDE
    final_from = core_of * HALF + column_of * 32 + step_of * CAP + final % CAP
    final_order = (final_from == slot_ids[None, :]).astype(jnp.bfloat16)

    got = [([], []), ([], [])]
    for hop in range(4):
        if hop == 2:
            blocks = reorder(after(final_order, got[0][0][1]), wide_back)
        for f in range(2):
            for side, steps in enumerate((z_shift(1), z_shift(-1))):
                if hop == 0:
                    block = packed[f][side]
                else:
                    block = got[f][side][-1][: CAPS[hop]]
                if hop == 1:
                    block = after(block, wide_rows)
                if hop == 2 and f == 1:
                    block = after(block, blocks[1])
                got[f][side].append(lax.ppermute(block, "z", steps))
    got = [rights + lefts for rights, lefts in got]
    last = [blocks[0]] + [None] * 7
    for steps, gate in (((1, 7), ()), ((2, 6), (1, 7)), ((3, 5, 4), (2, 6))):
        for step in steps:
            block = blocks[step]
            if gate:
                block = after(block, *[last[done] for done in gate])
            last[step] = lax.ppermute(block, "z", z_shift(step))

    slot_pick = slots(where, note, got[0])
    packed = repack(slot_pick, [own[0]] + got[0], [own[1]] + got[1])
    packed = after(packed, wide_back, last[1], last[7])
    arrived = lax.all_to_all(packed, CORE_WIDE, 0, 0, tiled=True)
    best = best_of(where, flag, gram(final_order, arrived), last)

    back = lax.all_to_all(best, ALL, 0, 0, tiled=True)
    failed = jnp.max(back) > 1e29
    mine = lax.dynamic_slice(back, (0, core * 64 + wide * CAP), (WORKERS, CAP))
    result = jnp.sum(
        jnp.where(back_place == slot_ids[:, None], mine.reshape(OUT)[:, None], 0.0), axis=0
    )
    return lax.cond(failed, padded_plan, lambda *_: result, embeddings, worker_of_row)


def solution(mesh):
    split = jax.sharding.Mesh(mesh.devices.reshape(PLANES, 2, WIDE), ALL)
    placed = (P(ALL, None), P(ALL, None))
    return jax.shard_map(
        on_device, mesh=split, in_specs=placed, out_specs=P(ALL), check_vma=False
    )
```

```python
import functools

import jax
import jax.numpy as jnp
from jax import lax
from jax.experimental import pallas as pl
from jax.experimental.pallas import tpu as pltpu
from jax.sharding import PartitionSpec as P

GRP = ("z", "core")
CORE_WIDE = ("core", "wide")
ALL = ("z", "core", "wide")
PLANES = 8
WIDE = 16
PER_PLANE = 32
WORKERS = 256
CAP = 4
HALF = 512
OUT = 1024
CAPS = (256, 192, 128, 64)
LIST = CAPS[0]
OWN_LIST = 128
Z_FIRST = (1280, 1024)
WIDE_FIRST = 1792
MARK = 2.0
REAL_MAX = 100.0
ROW_TILE = 256
NOTE = 1280
VMEM_LIMIT = 56 * 2**20


def padded_plan(embeddings, worker_of_row):
    row_count, features = embeddings.shape
    grp_count = lax.axis_size("z") * lax.axis_size("core")
    wide_count = lax.axis_size("wide")
    workers = grp_count * wide_count
    slot_count = workers * CAP
    values = embeddings.astype(jnp.float32)
    spread = jnp.mean(values * values, axis=1, keepdims=True)
    scaled = (values * lax.rsqrt(spread + 1e-06) * features ** (-0.25)).astype(jnp.bfloat16)
    target = worker_of_row[:, 0]
    matches = target[:, None] == jnp.arange(workers, dtype=jnp.int32)[None, :]
    one_hot = matches.astype(jnp.bfloat16)
    row_ids = jnp.arange(row_count, dtype=jnp.int32)
    earlier_mask = (row_ids[:, None] > row_ids[None, :]).astype(jnp.bfloat16)
    earlier = jnp.dot(earlier_mask, one_hot, preferred_element_type=jnp.float32)
    slot_index = jnp.sum(jnp.where(matches, earlier, 0.0), axis=1).astype(jnp.int32)
    sent_counts = jnp.sum(matches.astype(jnp.int32), axis=0)
    position = target * CAP + slot_index
    outgoing = jnp.zeros((slot_count, features), jnp.bfloat16).at[position].set(scaled)
    outgoing = outgoing.reshape(grp_count, wide_count, CAP, features)
    sent_counts = sent_counts.reshape(grp_count, wide_count, 1)

    def there(value):
        value = lax.all_to_all(value, GRP, split_axis=0, concat_axis=0, tiled=True)
        return lax.all_to_all(value, "wide", split_axis=1, concat_axis=1, tiled=True)

    arrived = there(outgoing).reshape(slot_count, features)
    counts_each = jnp.repeat(there(sent_counts).reshape(workers), CAP)
    slot_ids = jnp.arange(slot_count, dtype=jnp.int32)
    filled = slot_ids % CAP < counts_each
    paired = filled[:, None] & filled[None, :] & (slot_ids[:, None] != slot_ids[None, :])
    scores = lax.dot_general(
        arrived, arrived, (((1,), (1,)), ((), ())), preferred_element_type=jnp.float32
    )
    highest = jnp.max(jnp.where(paired, scores, -1e30), axis=1)
    back = highest.reshape(grp_count, wide_count, CAP)
    back = lax.all_to_all(back, "wide", split_axis=1, concat_axis=1, tiled=True)
    back = lax.all_to_all(back, GRP, split_axis=0, concat_axis=0, tiled=True)
    own_best = back.reshape(slot_count)[position]
    return jnp.where(own_best > -1e29, own_best, 0.0)


def z_shift(step):
    return [(z, (z + step) % PLANES) for z in range(PLANES)]


def after(value, *others):
    return lax.optimization_barrier((value,) + others)[0]


def call(kernel, out_shape, flops, **settings):
    return pl.pallas_call(
        kernel,
        out_shape=out_shape,
        compiler_params=pltpu.CompilerParams(vmem_limit_bytes=VMEM_LIMIT),
        cost_estimate=pl.CostEstimate(
            flops=flops, bytes_accessed=8 * 2**20, transcendentals=0
        ),
        **settings,
    )


def whole(value):
    return pl.BlockSpec(value.shape, lambda *_: (0,) * value.ndim)


def columns(rows, tile, first=0):
    return pl.BlockSpec((rows, tile), lambda i: (0, first + i))


def window(rows, tile, first):
    return pl.BlockSpec((pl.Element(rows), pl.Element(tile)), lambda i: (0, pl.multiple_of(first + i * tile, 128)))


def vmem():
    return pl.BlockSpec(memory_space=pltpu.VMEM)


def smem():
    return pl.BlockSpec(memory_space=pltpu.SMEM)


def iota(shape, axis):
    return lax.broadcasted_iota(jnp.int32, shape, axis)


def select_rows(pick, rows):
    return jnp.dot(pick, rows, preferred_element_type=jnp.float32)


def plan_kernel(
    where_ref,
    target_ref,
    x_ref,
    list_ref,
    wide_ref,
    fill_ref,
    note_ref,
    scale_ref,
    back_ref,
    flag_ref,
    squares,
):
    step = pl.program_id(0)
    f32, bf16 = jnp.float32, jnp.bfloat16
    part = jnp.zeros((HALF, 128), f32)
    for first in range(0, x_ref.shape[1], 128):
        values = x_ref[:, first : first + 128].astype(f32)
        part = part + values * values

    @pl.when(step == 0)
    def _():
        squares[...] = part
        z = where_ref[0]
        target = target_ref[...]
        across = (target == iota((WORKERS, HALF), 0)).astype(bf16)
        earlier = (iota((HALF, HALF), 0) < iota((HALF, HALF), 1)).astype(bf16)
        before = select_rows(across, earlier)
        counts = lax.dot_general(
            jnp.ones((16, HALF), bf16),
            across,
            (((1,), (1,)), ((), ())),
            preferred_element_type=f32,
        )
        down, over = iota((WORKERS, WORKERS), 0), iota((WORKERS, WORKERS), 1)
        same = down // PER_PLANE == over // PER_PLANE
        ahead = select_rows(counts.astype(bf16), (same & (down < over)).astype(bf16))[0:1, :]
        counts = counts[0:1, :]
        across = across.astype(f32)
        counts_down = jnp.sum(across, axis=1, keepdims=True)
        ahead_down = select_rows(
            (same & (over < down)).astype(bf16),
            jnp.broadcast_to(counts_down, (WORKERS, 128)).astype(bf16),
        )[:, 0:1]
        rank = jnp.sum(across * before, axis=0, keepdims=True).astype(jnp.int32)
        place = jnp.sum(across * (before + ahead_down), axis=0, keepdims=True).astype(jnp.int32)
        distance = (target // PER_PLANE - z) & (PLANES - 1)
        cluster_distance = (iota((1, WORKERS), 1) // PER_PLANE - z) & (PLANES - 1)
        n = [
            jnp.sum(jnp.where(cluster_distance == d, counts, 0.0), axis=1, keepdims=True).astype(
                jnp.int32
            )
            for d in range(PLANES)
        ]
        low = functools.reduce(
            jnp.maximum,
            (
                jnp.zeros_like(n[4]),
                n[4] - CAPS[3] + 1,
                n[4] + n[5] - CAPS[2] + 1,
                n[4] + n[5] + n[6] - CAPS[1] + 1,
                n[4] + n[5] + n[6] + n[7] - CAPS[0] + 1,
            ),
        )
        high = functools.reduce(
            jnp.minimum,
            (
                n[4],
                jnp.full_like(n[4], CAPS[3] - 1),
                CAPS[2] - 1 - n[3],
                CAPS[1] - 1 - n[3] - n[2],
                CAPS[0] - 1 - n[3] - n[2] - n[1],
            ),
        )
        to_right = jnp.clip((low + high) >> 1, 0, n[4])
        starts = [
            None,
            to_right + n[3] + n[2],
            to_right + n[3],
            to_right,
            to_right,
            n[4] - to_right,
            n[4] - to_right + n[5],
            n[4] - to_right + n[5] + n[6],
        ]

        def by_distance(which):
            value = jnp.zeros(which.shape, jnp.int32)
            for d in range(1, PLANES):
                value = jnp.where(which == d, starts[d], value)
            return value

        start = by_distance(distance)
        far_right = (distance == 4) & (place < to_right)
        far_left = (distance == 4) & (place >= to_right)
        goes_right = ((distance >= 1) & (distance <= 3)) | far_right
        on_list = jnp.where(far_right, place, jnp.where(far_left, place - to_right, start + place))
        list_place = jnp.where(
            distance == 0,
            2 * LIST + place,
            jnp.where(
                on_list >= LIST - 1, -1, jnp.where(goes_right, 1 + on_list, LIST + 1 + on_list)
            ),
        )
        list_ref[...] = (iota((2 * LIST + OWN_LIST, HALF), 0) == list_place).astype(bf16)
        wide_place = (target // WIDE % 2) * HALF + target % WIDE * 32 + distance * CAP + rank
        wide_match = (iota((OUT, HALF), 0) == wide_place).astype(f32)
        wide_ref[...] = wide_match.astype(bf16)
        fill_ref[...] = MARK * (1.0 - jnp.sum(wide_match, axis=1, keepdims=True))
        note_ref[...] = jnp.zeros((1, NOTE), f32)
        note_ref[:, 0:WORKERS] = counts
        note_ref[:, WORKERS : 2 * WORKERS] = ahead
        note_ref[:, 2 * WORKERS : 3 * WORKERS] = by_distance(cluster_distance).astype(f32)
        back_ref[...] = target * CAP + rank
        flag_ref[...] = jnp.broadcast_to((low > high).astype(f32), (1, 128))

    @pl.when(step > 0)
    def _():
        squares[...] += part

    @pl.when(step == pl.num_programs(0) - 1)
    def _():
        features = pl.num_programs(0) * x_ref.shape[1]
        spread = jnp.sum(squares[...], axis=1, keepdims=True) * (1.0 / features)
        scale_ref[...] = lax.rsqrt(spread + 1e-06) * features ** (-0.25)


def plan(where, targets, embeddings):
    f32, bf16 = jnp.float32, jnp.bfloat16
    shapes = [
        jax.ShapeDtypeStruct((2 * LIST + OWN_LIST, HALF), bf16),
        jax.ShapeDtypeStruct((OUT, HALF), bf16),
        jax.ShapeDtypeStruct((OUT, 1), f32),
        jax.ShapeDtypeStruct((1, NOTE), f32),
        jax.ShapeDtypeStruct((HALF, 1), f32),
        jax.ShapeDtypeStruct((1, HALF), jnp.int32),
        jax.ShapeDtypeStruct((1, 128), f32),
    ]
    return call(
        plan_kernel,
        shapes,
        10**9,
        grid=(4,),
        in_specs=[smem(), whole(targets), columns(HALF, embeddings.shape[1] // 4)],
        out_specs=[whole(shape) for shape in shapes],
        scratch_shapes=[pltpu.VMEM((HALF, 128), f32)],
    )(where, targets, embeddings)


def scaled_rows(x_ref, scale_ref):
    return (x_ref[...].astype(jnp.float32) * scale_ref[...]).astype(jnp.bfloat16)


def pack_lists_kernel(pick_ref, note_ref, scale_ref, x_ref, right_ref, left_ref, own_ref):
    packed = select_rows(pick_ref[...], scaled_rows(x_ref, scale_ref))
    first = iota((LIST, 1), 0) == 0
    note = note_ref[...]
    right_ref[...] = jnp.where(first, note, packed[0:LIST, :]).astype(jnp.bfloat16)
    left_ref[...] = jnp.where(first, note, packed[LIST : 2 * LIST, :]).astype(jnp.bfloat16)
    own_ref[...] = packed[2 * LIST :, :].astype(jnp.bfloat16)


def pack_lists(pick, note, scale, embeddings, first_column, width):
    tile = width // 2
    parts = (LIST, LIST, OWN_LIST)
    return call(
        pack_lists_kernel,
        [jax.ShapeDtypeStruct((rows, width), jnp.bfloat16) for rows in parts],
        2 * pick.shape[0] * HALF * width,
        grid=(width // tile,),
        in_specs=[
            whole(pick),
            columns(1, tile),
            whole(scale),
            window(HALF, tile, first_column),
        ],
        out_specs=[columns(rows, tile) for rows in parts],
    )(pick, note, scale, embeddings)


def pack_wide_kernel(pick_ref, fill_ref, scale_ref, x_ref, out_ref):
    packed = select_rows(pick_ref[...], scaled_rows(x_ref, scale_ref))
    out_ref[...] = (packed + fill_ref[...]).astype(jnp.bfloat16)


def pack_wide(pick, fill, scale, embeddings, first_column, width):
    tile = width // 2
    return call(
        pack_wide_kernel,
        jax.ShapeDtypeStruct((OUT, width), jnp.bfloat16),
        2 * OUT * HALF * width,
        grid=(width // tile,),
        in_specs=[
            whole(pick),
            whole(fill),
            whole(scale),
            window(HALF, tile, first_column),
        ],
        out_specs=columns(OUT, tile),
    )(pick, fill, scale, embeddings)


def reorder_kernel(pick_ref, x_ref, *out_refs):
    moved = select_rows(pick_ref[...], x_ref[...]).astype(jnp.bfloat16)
    for index, out_ref in enumerate(out_refs):
        out_ref[...] = moved[index * 128 : index * 128 + 128, :]


def reorder(pick, value):
    width = value.shape[1]
    tile = 256
    return call(
        reorder_kernel,
        [jax.ShapeDtypeStruct((128, width), jnp.bfloat16)] * PLANES,
        2 * OUT * OUT * width,
        grid=(width // tile,),
        in_specs=[whole(pick), columns(OUT, tile)],
        out_specs=[columns(128, tile)] * PLANES,
    )(pick, value)


def slots_kernel(where_ref, note_ref, *refs):
    firsts, out_ref, told = refs[:-2], refs[-2], refs[-1]
    told[...] = jnp.zeros(told.shape, jnp.float32)
    told[0:1, :] = note_ref[...]
    for index, first in enumerate(firsts):
        told[index + 1 : index + 2, :] = first[...].astype(jnp.float32)[0:1, :]
    slot = iota((OUT, 1), 0)
    step, rank = slot // CAP % PLANES, slot % CAP
    by_step = (iota((OUT, 16), 1) == step).astype(jnp.bfloat16)
    mine = iota((OUT, WORKERS), 1) == where_ref[0] * PER_PLANE + slot // 32

    def heard(index):
        told_here = told[:, index * WORKERS : index * WORKERS + WORKERS].astype(jnp.bfloat16)
        value = jnp.where(mine, select_rows(by_step, told_here), 0.0)
        return jnp.sum(value, axis=1, keepdims=True).astype(jnp.int32)

    count, place, start = heard(0), heard(1) + rank, heard(2)
    offsets = [OWN_LIST]
    for cap in CAPS + CAPS:
        offsets.append(offsets[-1] + cap)
    found = jnp.where(
        place < start, offsets[3] + 1 + place, offsets[7] + 1 + place - start
    )
    for d, block in ((1, 0), (2, 1), (3, 2), (5, 6), (6, 5), (7, 4)):
        found = jnp.where(step == d, offsets[block] + 1 + start + place, found)
    found = jnp.where(step == 0, place, found)
    found = jnp.where(rank < count, found, -1)
    out_ref[...] = (found == iota(out_ref.shape, 1)).astype(jnp.bfloat16)


def slots(where, note, blocks):
    firsts = [blocks[b] for b in (0, 1, 2, 3, 6, 5, 4)]
    shape = jax.ShapeDtypeStruct((OUT, OWN_LIST + 2 * sum(CAPS)), jnp.bfloat16)
    return call(
        slots_kernel,
        shape,
        10**9,
        grid=(1,),
        in_specs=[smem(), whole(note)]
        + [pl.BlockSpec((16, NOTE), lambda i: (0, 0)) for _ in firsts],
        out_specs=whole(shape),
        scratch_shapes=[pltpu.VMEM((16, NOTE), jnp.float32)],
    )(where, note, *firsts)


def repack_kernel(turn, pick_ref, *refs):
    blocks, out_ref, held = refs[:-2], refs[-2], refs[-1]
    step = pl.program_id(0)
    for chunk in range(2):

        @pl.when((step >= turn) == bool(chunk))
        def _(chunk=chunk):
            first = pl.multiple_of((step - chunk * turn) * 256, 256)
            base = 0
            for block in blocks[chunk * 9 : chunk * 9 + 9]:
                rows = block.shape[0]
                held[base : base + rows, :] = block[:, pl.ds(first, 256)]
                base += rows

    out_ref[...] = select_rows(pick_ref[...], held[...]).astype(jnp.bfloat16)


def repack(pick, first_blocks, second_blocks):
    tile = 256
    depth = pick.shape[1]
    turn = first_blocks[0].shape[1] // tile
    steps = turn + second_blocks[0].shape[1] // tile
    blocks = list(first_blocks) + list(second_blocks)
    return call(
        functools.partial(repack_kernel, turn),
        jax.ShapeDtypeStruct((OUT, steps * tile), jnp.bfloat16),
        2 * OUT * depth * steps * tile,
        grid=(steps,),
        in_specs=[whole(value) for value in [pick] + blocks],
        out_specs=columns(OUT, tile),
        scratch_shapes=[pltpu.VMEM((depth, tile), jnp.bfloat16)],
    )(pick, *blocks)


def gram_kernel(pick_ref, x_ref, out_ref, held):
    step = pl.program_id(0)
    held[step] = select_rows(pick_ref[...], x_ref[...]).astype(jnp.bfloat16)

    @pl.when(step == pl.num_programs(0) - 1)
    def _():
        for tile in range(0, OUT, ROW_TILE):
            part = 0.0
            for index in range(held.shape[0]):
                part = part + lax.dot_general(
                    held[index, tile : tile + ROW_TILE, :],
                    held[index],
                    (((1,), (1,)), ((), ())),
                    preferred_element_type=jnp.float32,
                )
            out_ref[tile : tile + ROW_TILE, :] = part


def gram(pick, value):
    width = value.shape[1]
    tile = 768
    return call(
        gram_kernel,
        jax.ShapeDtypeStruct((OUT, OUT), jnp.float32),
        4 * OUT * OUT * width,
        grid=(width // tile,),
        in_specs=[whole(pick), columns(OUT, tile)],
        out_specs=pl.BlockSpec((OUT, OUT), lambda i: (0, 0)),
        scratch_shapes=[pltpu.VMEM((width // tile, OUT, tile), jnp.bfloat16)],
    )(pick, value)


def best_kernel(where_ref, flag_ref, total_ref, *refs):
    blocks, out_ref, held, best_ref = refs[:PLANES], refs[PLANES], refs[-2], refs[-1]
    step = pl.program_id(0)

    @pl.when(step == 0)
    def _():
        for index, block in enumerate(blocks):
            held[index * 128 : index * 128 + 128, :] = block[...]
        best_ref[...] = jnp.full((1, OUT), -1e30, jnp.float32)

    first = pl.multiple_of(step * ROW_TILE, ROW_TILE)
    part = total_ref[...] + lax.dot_general(
        held[pl.ds(first, ROW_TILE), :],
        held[...],
        (((1,), (1,)), ((), ())),
        preferred_element_type=jnp.float32,
    )
    same = first + iota((ROW_TILE, OUT), 0) == iota((ROW_TILE, OUT), 1)
    squares = jnp.sum(jnp.where(same, part, 0.0), axis=1, keepdims=True)
    closed = same | (squares >= REAL_MAX)
    best = jnp.maximum(
        best_ref[...], jnp.max(jnp.where(closed, -1e30, part), axis=0, keepdims=True)
    )
    best_ref[...] = best

    @pl.when(step == pl.num_programs(0) - 1)
    def _():
        result = jnp.where(best > -1e29, best, 0.0)
        result = jnp.where(flag_ref[0:1, 0:1] > 0.5, 1e30, result)
        for d in range(PLANES):
            plane = (where_ref[0] - d) & (PLANES - 1)
            out_ref[pl.ds(pl.multiple_of(plane * 32, 32), 32), :] = jnp.broadcast_to(
                result[:, d * 128 : d * 128 + 128], (32, 128)
            )


def best_of(where, flag, total, blocks):
    width = blocks[0].shape[1]
    shape = jax.ShapeDtypeStruct((WORKERS, 128), jnp.float32)
    return call(
        best_kernel,
        shape,
        2 * OUT * OUT * width,
        grid=(OUT // ROW_TILE,),
        in_specs=[smem(), whole(flag), pl.BlockSpec((ROW_TILE, OUT), lambda i: (i, 0))]
        + [whole(block) for block in blocks],
        out_specs=whole(shape),
        scratch_shapes=[
            pltpu.VMEM((OUT, width), jnp.bfloat16),
            pltpu.VMEM((1, OUT), jnp.float32),
        ],
    )(where, flag, total, *blocks)


def on_device(embeddings, worker_of_row):
    i32 = jnp.int32
    core = lax.axis_index("core")
    wide = lax.axis_index("wide")
    where = lax.axis_index("z").astype(i32).reshape(1)
    list_pick, wide_pick, wide_fill, note, scale, back_place, flag = plan(
        where, worker_of_row.reshape(1, HALF), embeddings
    )

    packed, own = [], []
    for f in range(2):
        right, left, mine = pack_lists(
            list_pick, note, scale, embeddings, sum(Z_FIRST[:f]), Z_FIRST[f]
        )
        packed.append((right, left))
        own.append(mine)

    wide_rows = pack_wide(
        after(wide_pick, packed[0][0]), wide_fill, scale, embeddings, sum(Z_FIRST), WIDE_FIRST
    )
    wide_back = lax.all_to_all(wide_rows, CORE_WIDE, 0, 0, tiled=True)

    slot_ids = jnp.arange(OUT, dtype=i32)
    final = slot_ids[:, None]
    step_of, core_of, column_of = final // 128, final // 64 % 2, final // 4 % WIDE
    final_from = core_of * HALF + column_of * 32 + step_of * CAP + final % CAP
    final_order = (final_from == slot_ids[None, :]).astype(jnp.bfloat16)

    got = [([], []), ([], [])]
    for hop in range(4):
        if hop == 2:
            blocks = reorder(after(final_order, got[0][0][1]), wide_back)
        for f in range(2):
            for side, steps in enumerate((z_shift(1), z_shift(-1))):
                if hop == 0:
                    block = packed[f][side]
                else:
                    block = got[f][side][-1][: CAPS[hop]]
                if hop == 1:
                    block = after(block, wide_rows)
                if 1 <= hop <= 2 and f == 1:
                    block = after(block, got[0][side][hop])
                if hop == 3 and f == 0:
                    block = after(block, blocks[1])
                got[f][side].append(lax.ppermute(block, "z", steps))
    got = [rights + lefts for rights, lefts in got]
    last = [blocks[0]] + [None] * 7
    for steps, gate in (((1, 7), ()), ((2, 6), (1, 7)), ((3, 5, 4), (2, 6))):
        for step in steps:
            block = blocks[step]
            if gate:
                block = after(block, *[last[done] for done in gate])
            last[step] = lax.ppermute(block, "z", z_shift(step))

    slot_pick = slots(where, note, got[0])
    packed = repack(slot_pick, [own[0]] + got[0], [own[1]] + got[1])
    packed = after(packed, wide_back, last[1], last[7])
    arrived = lax.all_to_all(packed, CORE_WIDE, 0, 0, tiled=True)
    best = best_of(where, flag, gram(final_order, arrived), last)

    back = lax.all_to_all(best, ALL, 0, 0, tiled=True)
    failed = jnp.max(back) > 1e29
    mine = lax.dynamic_slice(back, (0, core * 64 + wide * CAP), (WORKERS, CAP))
    result = jnp.sum(
        jnp.where(back_place == slot_ids[:, None], mine.reshape(OUT)[:, None], 0.0), axis=0
    )
    return lax.cond(failed, padded_plan, lambda *_: result, embeddings, worker_of_row)


def solution(mesh):
    split = jax.sharding.Mesh(mesh.devices.reshape(PLANES, 2, WIDE), ALL)
    placed = (P(ALL, None), P(ALL, None))
    return jax.shard_map(
        on_device, mesh=split, in_specs=placed, out_specs=P(ALL), check_vma=False
    )
```

```python
import functools

import jax
import jax.numpy as jnp
from jax import lax
from jax.experimental import pallas as pl
from jax.experimental.pallas import tpu as pltpu
from jax.sharding import PartitionSpec as P

GRP = ("z", "core")
CORE_WIDE = ("core", "wide")
ALL = ("z", "core", "wide")
PLANES = 8
WIDE = 16
PER_PLANE = 32
WORKERS = 256
CAP = 4
HALF = 512
OUT = 1024
CAPS = (256, 192, 128, 64)
LIST = CAPS[0]
OWN_LIST = 128
Z_FIRST = (1280, 1024)
WIDE_FIRST = 1792
MARK = 2.0
REAL_MAX = 100.0
ROW_TILE = 256
NOTE = 1280
VMEM_LIMIT = 56 * 2**20


def padded_plan(embeddings, worker_of_row):
    row_count, features = embeddings.shape
    grp_count = lax.axis_size("z") * lax.axis_size("core")
    wide_count = lax.axis_size("wide")
    workers = grp_count * wide_count
    slot_count = workers * CAP
    values = embeddings.astype(jnp.float32)
    spread = jnp.mean(values * values, axis=1, keepdims=True)
    scaled = (values * lax.rsqrt(spread + 1e-06) * features ** (-0.25)).astype(jnp.bfloat16)
    target = worker_of_row[:, 0]
    matches = target[:, None] == jnp.arange(workers, dtype=jnp.int32)[None, :]
    one_hot = matches.astype(jnp.bfloat16)
    row_ids = jnp.arange(row_count, dtype=jnp.int32)
    earlier_mask = (row_ids[:, None] > row_ids[None, :]).astype(jnp.bfloat16)
    earlier = jnp.dot(earlier_mask, one_hot, preferred_element_type=jnp.float32)
    slot_index = jnp.sum(jnp.where(matches, earlier, 0.0), axis=1).astype(jnp.int32)
    sent_counts = jnp.sum(matches.astype(jnp.int32), axis=0)
    position = target * CAP + slot_index
    outgoing = jnp.zeros((slot_count, features), jnp.bfloat16).at[position].set(scaled)
    outgoing = outgoing.reshape(grp_count, wide_count, CAP, features)
    sent_counts = sent_counts.reshape(grp_count, wide_count, 1)

    def there(value):
        value = lax.all_to_all(value, GRP, split_axis=0, concat_axis=0, tiled=True)
        return lax.all_to_all(value, "wide", split_axis=1, concat_axis=1, tiled=True)

    arrived = there(outgoing).reshape(slot_count, features)
    counts_each = jnp.repeat(there(sent_counts).reshape(workers), CAP)
    slot_ids = jnp.arange(slot_count, dtype=jnp.int32)
    filled = slot_ids % CAP < counts_each
    paired = filled[:, None] & filled[None, :] & (slot_ids[:, None] != slot_ids[None, :])
    scores = lax.dot_general(
        arrived, arrived, (((1,), (1,)), ((), ())), preferred_element_type=jnp.float32
    )
    highest = jnp.max(jnp.where(paired, scores, -1e30), axis=1)
    back = highest.reshape(grp_count, wide_count, CAP)
    back = lax.all_to_all(back, "wide", split_axis=1, concat_axis=1, tiled=True)
    back = lax.all_to_all(back, GRP, split_axis=0, concat_axis=0, tiled=True)
    own_best = back.reshape(slot_count)[position]
    return jnp.where(own_best > -1e29, own_best, 0.0)


def z_shift(step):
    return [(z, (z + step) % PLANES) for z in range(PLANES)]


def after(value, *others):
    return lax.optimization_barrier((value,) + others)[0]


def call(kernel, out_shape, flops, **settings):
    return pl.pallas_call(
        kernel,
        out_shape=out_shape,
        compiler_params=pltpu.CompilerParams(vmem_limit_bytes=VMEM_LIMIT),
        cost_estimate=pl.CostEstimate(
            flops=flops, bytes_accessed=8 * 2**20, transcendentals=0
        ),
        **settings,
    )


def whole(value):
    return pl.BlockSpec(value.shape, lambda *_: (0,) * value.ndim)


def columns(rows, tile, first=0):
    return pl.BlockSpec((rows, tile), lambda i: (0, first + i))


def window(rows, tile, first):
    return pl.BlockSpec((pl.Element(rows), pl.Element(tile)), lambda i: (0, pl.multiple_of(first + i * tile, 128)))


def vmem():
    return pl.BlockSpec(memory_space=pltpu.VMEM)


def smem():
    return pl.BlockSpec(memory_space=pltpu.SMEM)


def iota(shape, axis):
    return lax.broadcasted_iota(jnp.int32, shape, axis)


def select_rows(pick, rows):
    return jnp.dot(pick, rows, preferred_element_type=jnp.float32)


def plan_kernel(
    where_ref,
    target_ref,
    x_ref,
    list_ref,
    wide_ref,
    fill_ref,
    note_ref,
    scale_ref,
    back_ref,
    flag_ref,
    squares,
):
    step = pl.program_id(0)
    f32, bf16 = jnp.float32, jnp.bfloat16
    part = jnp.zeros((HALF, 128), f32)
    for first in range(0, x_ref.shape[1], 128):
        values = x_ref[:, first : first + 128].astype(f32)
        part = part + values * values

    @pl.when(step == 0)
    def _():
        squares[...] = part
        z = where_ref[0]
        target = target_ref[...]
        across = (target == iota((WORKERS, HALF), 0)).astype(bf16)
        earlier = (iota((HALF, HALF), 0) < iota((HALF, HALF), 1)).astype(bf16)
        before = select_rows(across, earlier)
        counts = lax.dot_general(
            jnp.ones((16, HALF), bf16),
            across,
            (((1,), (1,)), ((), ())),
            preferred_element_type=f32,
        )
        down, over = iota((WORKERS, WORKERS), 0), iota((WORKERS, WORKERS), 1)
        same = down // PER_PLANE == over // PER_PLANE
        ahead = select_rows(counts.astype(bf16), (same & (down < over)).astype(bf16))[0:1, :]
        counts = counts[0:1, :]
        across = across.astype(f32)
        counts_down = jnp.sum(across, axis=1, keepdims=True)
        ahead_down = select_rows(
            (same & (over < down)).astype(bf16),
            jnp.broadcast_to(counts_down, (WORKERS, 128)).astype(bf16),
        )[:, 0:1]
        rank = jnp.sum(across * before, axis=0, keepdims=True).astype(jnp.int32)
        place = jnp.sum(across * (before + ahead_down), axis=0, keepdims=True).astype(jnp.int32)
        distance = (target // PER_PLANE - z) & (PLANES - 1)
        cluster_distance = (iota((1, WORKERS), 1) // PER_PLANE - z) & (PLANES - 1)
        n = [
            jnp.sum(jnp.where(cluster_distance == d, counts, 0.0), axis=1, keepdims=True).astype(
                jnp.int32
            )
            for d in range(PLANES)
        ]
        low = functools.reduce(
            jnp.maximum,
            (
                jnp.zeros_like(n[4]),
                n[4] - CAPS[3] + 1,
                n[4] + n[5] - CAPS[2] + 1,
                n[4] + n[5] + n[6] - CAPS[1] + 1,
                n[4] + n[5] + n[6] + n[7] - CAPS[0] + 1,
            ),
        )
        high = functools.reduce(
            jnp.minimum,
            (
                n[4],
                jnp.full_like(n[4], CAPS[3] - 1),
                CAPS[2] - 1 - n[3],
                CAPS[1] - 1 - n[3] - n[2],
                CAPS[0] - 1 - n[3] - n[2] - n[1],
            ),
        )
        to_right = jnp.clip((low + high) >> 1, 0, n[4])
        starts = [
            None,
            to_right + n[3] + n[2],
            to_right + n[3],
            to_right,
            to_right,
            n[4] - to_right,
            n[4] - to_right + n[5],
            n[4] - to_right + n[5] + n[6],
        ]

        def by_distance(which):
            value = jnp.zeros(which.shape, jnp.int32)
            for d in range(1, PLANES):
                value = jnp.where(which == d, starts[d], value)
            return value

        start = by_distance(distance)
        far_right = (distance == 4) & (place < to_right)
        far_left = (distance == 4) & (place >= to_right)
        goes_right = ((distance >= 1) & (distance <= 3)) | far_right
        on_list = jnp.where(far_right, place, jnp.where(far_left, place - to_right, start + place))
        list_place = jnp.where(
            distance == 0,
            2 * LIST + place,
            jnp.where(
                on_list >= LIST - 1, -1, jnp.where(goes_right, 1 + on_list, LIST + 1 + on_list)
            ),
        )
        list_ref[...] = (iota((2 * LIST + OWN_LIST, HALF), 0) == list_place).astype(bf16)
        wide_place = (target // WIDE % 2) * HALF + target % WIDE * 32 + distance * CAP + rank
        wide_match = (iota((OUT, HALF), 0) == wide_place).astype(f32)
        wide_ref[...] = wide_match.astype(bf16)
        fill_ref[...] = MARK * (1.0 - jnp.sum(wide_match, axis=1, keepdims=True))
        note_ref[...] = jnp.zeros((1, NOTE), f32)
        note_ref[:, 0:WORKERS] = counts
        note_ref[:, WORKERS : 2 * WORKERS] = ahead
        note_ref[:, 2 * WORKERS : 3 * WORKERS] = by_distance(cluster_distance).astype(f32)
        back_ref[...] = target * CAP + rank
        flag_ref[...] = jnp.broadcast_to((low > high).astype(f32), (1, 128))

    @pl.when(step > 0)
    def _():
        squares[...] += part

    @pl.when(step == pl.num_programs(0) - 1)
    def _():
        features = pl.num_programs(0) * x_ref.shape[1]
        spread = jnp.sum(squares[...], axis=1, keepdims=True) * (1.0 / features)
        scale_ref[...] = lax.rsqrt(spread + 1e-06) * features ** (-0.25)


def plan(where, targets, embeddings):
    f32, bf16 = jnp.float32, jnp.bfloat16
    shapes = [
        jax.ShapeDtypeStruct((2 * LIST + OWN_LIST, HALF), bf16),
        jax.ShapeDtypeStruct((OUT, HALF), bf16),
        jax.ShapeDtypeStruct((OUT, 1), f32),
        jax.ShapeDtypeStruct((1, NOTE), f32),
        jax.ShapeDtypeStruct((HALF, 1), f32),
        jax.ShapeDtypeStruct((1, HALF), jnp.int32),
        jax.ShapeDtypeStruct((1, 128), f32),
    ]
    return call(
        plan_kernel,
        shapes,
        10**9,
        grid=(4,),
        in_specs=[smem(), whole(targets), columns(HALF, embeddings.shape[1] // 4)],
        out_specs=[whole(shape) for shape in shapes],
        scratch_shapes=[pltpu.VMEM((HALF, 128), f32)],
    )(where, targets, embeddings)


def scaled_rows(x_ref, scale_ref):
    return (x_ref[...].astype(jnp.float32) * scale_ref[...]).astype(jnp.bfloat16)


def pack_lists_kernel(pick_ref, note_ref, scale_ref, x_ref, right_ref, left_ref, own_ref):
    packed = select_rows(pick_ref[...], scaled_rows(x_ref, scale_ref))
    first = iota((LIST, 1), 0) == 0
    note = note_ref[...]
    right_ref[...] = jnp.where(first, note, packed[0:LIST, :]).astype(jnp.bfloat16)
    left_ref[...] = jnp.where(first, note, packed[LIST : 2 * LIST, :]).astype(jnp.bfloat16)
    own_ref[...] = packed[2 * LIST :, :].astype(jnp.bfloat16)


def pack_lists(pick, note, scale, embeddings, first_column, width):
    tile = width // 2
    parts = (LIST, LIST, OWN_LIST)
    return call(
        pack_lists_kernel,
        [jax.ShapeDtypeStruct((rows, width), jnp.bfloat16) for rows in parts],
        2 * pick.shape[0] * HALF * width,
        grid=(width // tile,),
        in_specs=[
            whole(pick),
            columns(1, tile),
            whole(scale),
            window(HALF, tile, first_column),
        ],
        out_specs=[columns(rows, tile) for rows in parts],
    )(pick, note, scale, embeddings)


def pack_wide_kernel(pick_ref, fill_ref, scale_ref, x_ref, out_ref):
    packed = select_rows(pick_ref[...], scaled_rows(x_ref, scale_ref))
    out_ref[...] = (packed + fill_ref[...]).astype(jnp.bfloat16)


def pack_wide(pick, fill, scale, embeddings, first_column, width):
    tile = width // 2
    return call(
        pack_wide_kernel,
        jax.ShapeDtypeStruct((OUT, width), jnp.bfloat16),
        2 * OUT * HALF * width,
        grid=(width // tile,),
        in_specs=[
            whole(pick),
            whole(fill),
            whole(scale),
            window(HALF, tile, first_column),
        ],
        out_specs=columns(OUT, tile),
    )(pick, fill, scale, embeddings)


def reorder_kernel(pick_ref, x_ref, *out_refs):
    moved = select_rows(pick_ref[...], x_ref[...]).astype(jnp.bfloat16)
    for index, out_ref in enumerate(out_refs):
        out_ref[...] = moved[index * 128 : index * 128 + 128, :]


def reorder(pick, value):
    width = value.shape[1]
    tile = 256
    return call(
        reorder_kernel,
        [jax.ShapeDtypeStruct((128, width), jnp.bfloat16)] * PLANES,
        2 * OUT * OUT * width,
        grid=(width // tile,),
        in_specs=[whole(pick), columns(OUT, tile)],
        out_specs=[columns(128, tile)] * PLANES,
    )(pick, value)


def slots_kernel(where_ref, note_ref, *refs):
    firsts, out_ref, told = refs[:-2], refs[-2], refs[-1]
    told[...] = jnp.zeros(told.shape, jnp.float32)
    told[0:1, :] = note_ref[...]
    for index, first in enumerate(firsts):
        told[index + 1 : index + 2, :] = first[...].astype(jnp.float32)[0:1, :]
    slot = iota((OUT, 1), 0)
    step, rank = slot // CAP % PLANES, slot % CAP
    by_step = (iota((OUT, 16), 1) == step).astype(jnp.bfloat16)
    mine = iota((OUT, WORKERS), 1) == where_ref[0] * PER_PLANE + slot // 32

    def heard(index):
        told_here = told[:, index * WORKERS : index * WORKERS + WORKERS].astype(jnp.bfloat16)
        value = jnp.where(mine, select_rows(by_step, told_here), 0.0)
        return jnp.sum(value, axis=1, keepdims=True).astype(jnp.int32)

    count, place, start = heard(0), heard(1) + rank, heard(2)
    offsets = [OWN_LIST]
    for cap in CAPS + CAPS:
        offsets.append(offsets[-1] + cap)
    found = jnp.where(
        place < start, offsets[3] + 1 + place, offsets[7] + 1 + place - start
    )
    for d, block in ((1, 0), (2, 1), (3, 2), (5, 6), (6, 5), (7, 4)):
        found = jnp.where(step == d, offsets[block] + 1 + start + place, found)
    found = jnp.where(step == 0, place, found)
    found = jnp.where(rank < count, found, -1)
    out_ref[...] = (found == iota(out_ref.shape, 1)).astype(jnp.bfloat16)


def slots(where, note, blocks):
    firsts = [blocks[b] for b in (0, 1, 2, 3, 6, 5, 4)]
    shape = jax.ShapeDtypeStruct((OUT, OWN_LIST + 2 * sum(CAPS)), jnp.bfloat16)
    return call(
        slots_kernel,
        shape,
        10**9,
        grid=(1,),
        in_specs=[smem(), whole(note)]
        + [pl.BlockSpec((16, NOTE), lambda i: (0, 0)) for _ in firsts],
        out_specs=whole(shape),
        scratch_shapes=[pltpu.VMEM((16, NOTE), jnp.float32)],
    )(where, note, *firsts)


def repack_kernel(turn, pick_ref, *refs):
    blocks, out_ref, held = refs[:-2], refs[-2], refs[-1]
    step = pl.program_id(0)
    for chunk in range(2):

        @pl.when((step >= turn) == bool(chunk))
        def _(chunk=chunk):
            first = pl.multiple_of((step - chunk * turn) * 256, 256)
            base = 0
            for block in blocks[chunk * 9 : chunk * 9 + 9]:
                rows = block.shape[0]
                held[base : base + rows, :] = block[:, pl.ds(first, 256)]
                base += rows

    out_ref[...] = select_rows(pick_ref[...], held[...]).astype(jnp.bfloat16)


def repack(pick, first_blocks, second_blocks):
    tile = 256
    depth = pick.shape[1]
    turn = first_blocks[0].shape[1] // tile
    steps = turn + second_blocks[0].shape[1] // tile
    blocks = list(first_blocks) + list(second_blocks)
    return call(
        functools.partial(repack_kernel, turn),
        jax.ShapeDtypeStruct((OUT, steps * tile), jnp.bfloat16),
        2 * OUT * depth * steps * tile,
        grid=(steps,),
        in_specs=[whole(value) for value in [pick] + blocks],
        out_specs=columns(OUT, tile),
        scratch_shapes=[pltpu.VMEM((depth, tile), jnp.bfloat16)],
    )(pick, *blocks)


def gram_kernel(pick_ref, x_ref, out_ref, held):
    step = pl.program_id(0)
    held[step] = select_rows(pick_ref[...], x_ref[...]).astype(jnp.bfloat16)

    @pl.when(step == pl.num_programs(0) - 1)
    def _():
        for tile in range(0, OUT, ROW_TILE):
            part = 0.0
            for index in range(held.shape[0]):
                part = part + lax.dot_general(
                    held[index, tile : tile + ROW_TILE, :],
                    held[index, tile:, :],
                    (((1,), (1,)), ((), ())),
                    preferred_element_type=jnp.float32,
                )
            out_ref[tile : tile + ROW_TILE, tile:] = part


def gram(pick, value):
    width = value.shape[1]
    tile = 768
    return call(
        gram_kernel,
        jax.ShapeDtypeStruct((OUT, OUT), jnp.float32),
        4 * OUT * OUT * width,
        grid=(width // tile,),
        in_specs=[whole(pick), columns(OUT, tile)],
        out_specs=pl.BlockSpec((OUT, OUT), lambda i: (0, 0)),
        scratch_shapes=[pltpu.VMEM((width // tile, OUT, tile), jnp.bfloat16)],
    )(pick, value)


def best_kernel(where_ref, flag_ref, total_ref, *refs):
    blocks, out_ref, held = refs[:PLANES], refs[PLANES], refs[-1]
    for index, block in enumerate(blocks):
        held[index * 128 : index * 128 + 128, :] = block[...]
    count = OUT // ROW_TILE
    same = iota((ROW_TILE, ROW_TILE), 0) == iota((ROW_TILE, ROW_TILE), 1)
    best = [jnp.full((1, ROW_TILE), -1e30, jnp.float32)] * count
    filled = [None] * count
    for tile in reversed(range(count)):
        first = tile * ROW_TILE
        part = total_ref[first : first + ROW_TILE, first:] + lax.dot_general(
            held[first : first + ROW_TILE, :],
            held[first:, :],
            (((1,), (1,)), ((), ())),
            preferred_element_type=jnp.float32,
        )
        diagonal = jnp.where(same, part[:, :ROW_TILE], 0.0)
        row_filled = jnp.sum(diagonal, axis=1, keepdims=True) < REAL_MAX
        filled[tile] = jnp.sum(diagonal, axis=0, keepdims=True) < REAL_MAX
        across = jnp.full((ROW_TILE, 1), -1e30, jnp.float32)
        for other in range(tile, count):
            scores = part[:, (other - tile) * ROW_TILE : (other - tile + 1) * ROW_TILE]
            allowed = row_filled & jnp.logical_not(same) if other == tile else row_filled
            down = jnp.max(jnp.where(allowed, scores, -1e30), axis=0, keepdims=True)
            best[other] = jnp.maximum(best[other], down)
            if other > tile:
                most = jnp.max(jnp.where(filled[other], scores, -1e30), axis=1, keepdims=True)
                across = jnp.maximum(across, most)
        turned = jnp.sum(jnp.where(same, across, 0.0), axis=0, keepdims=True)
        best[tile] = jnp.maximum(best[tile], turned)
    for d in range(PLANES):
        result = best[d // 2][:, d % 2 * 128 : d % 2 * 128 + 128]
        result = jnp.where(result > -1e29, result, 0.0)
        result = jnp.where(flag_ref[0:1, 0:1] > 0.5, 1e30, result)
        plane = (where_ref[0] - d) & (PLANES - 1)
        out_ref[pl.ds(pl.multiple_of(plane * 32, 32), 32), :] = jnp.broadcast_to(
            result, (32, 128)
        )


def best_of(where, flag, total, blocks):
    width = blocks[0].shape[1]
    shape = jax.ShapeDtypeStruct((WORKERS, 128), jnp.float32)
    return call(
        best_kernel,
        shape,
        2 * OUT * OUT * width,
        grid=(1,),
        in_specs=[smem()] + [whole(value) for value in [flag, total] + blocks],
        out_specs=whole(shape),
        scratch_shapes=[pltpu.VMEM((OUT, width), jnp.bfloat16)],
    )(where, flag, total, *blocks)


def on_device(embeddings, worker_of_row):
    i32 = jnp.int32
    core = lax.axis_index("core")
    wide = lax.axis_index("wide")
    where = lax.axis_index("z").astype(i32).reshape(1)
    list_pick, wide_pick, wide_fill, note, scale, back_place, flag = plan(
        where, worker_of_row.reshape(1, HALF), embeddings
    )

    packed, own = [], []
    for f in range(2):
        right, left, mine = pack_lists(
            list_pick, note, scale, embeddings, sum(Z_FIRST[:f]), Z_FIRST[f]
        )
        packed.append((right, left))
        own.append(mine)

    wide_rows = pack_wide(
        after(wide_pick, packed[0][0]), wide_fill, scale, embeddings, sum(Z_FIRST), WIDE_FIRST
    )
    wide_back = lax.all_to_all(wide_rows, CORE_WIDE, 0, 0, tiled=True)

    slot_ids = jnp.arange(OUT, dtype=i32)
    final = slot_ids[:, None]
    step_of, core_of, column_of = final // 128, final // 64 % 2, final // 4 % WIDE
    final_from = core_of * HALF + column_of * 32 + step_of * CAP + final % CAP
    final_order = (final_from == slot_ids[None, :]).astype(jnp.bfloat16)

    got = [([], []), ([], [])]
    for hop in range(4):
        if hop == 2:
            blocks = reorder(after(final_order, got[0][0][1]), wide_back)
        for f in range(2):
            for side, steps in enumerate((z_shift(1), z_shift(-1))):
                if hop == 0:
                    block = packed[f][side]
                else:
                    block = got[f][side][-1][: CAPS[hop]]
                if hop == 1:
                    block = after(block, wide_rows)
                if hop == 2 and f == 1:
                    block = after(block, blocks[1])
                got[f][side].append(lax.ppermute(block, "z", steps))
    got = [rights + lefts for rights, lefts in got]
    last = [blocks[0]] + [None] * 7
    for steps, gate in (((2, 6), ()), ((1, 7, 4), (2, 6)), ((3, 5), (1, 7))):
        for step in steps:
            block = blocks[step]
            if gate:
                block = after(block, *[last[done] for done in gate])
            last[step] = lax.ppermute(block, "z", z_shift(step))

    slot_pick = slots(where, note, got[0])
    packed = repack(slot_pick, [own[0]] + got[0], [own[1]] + got[1])
    packed = after(packed, wide_back, last[2], last[6])
    arrived = lax.all_to_all(packed, CORE_WIDE, 0, 0, tiled=True)
    best = best_of(where, flag, gram(final_order, arrived), last)

    back = lax.all_to_all(best, ALL, 0, 0, tiled=True)
    failed = jnp.max(back) > 1e29
    mine = lax.dynamic_slice(back, (0, core * 64 + wide * CAP), (WORKERS, CAP))
    result = jnp.sum(
        jnp.where(back_place == slot_ids[:, None], mine.reshape(OUT)[:, None], 0.0), axis=0
    )
    return lax.cond(failed, padded_plan, lambda *_: result, embeddings, worker_of_row)


def solution(mesh):
    split = jax.sharding.Mesh(mesh.devices.reshape(PLANES, 2, WIDE), ALL)
    placed = (P(ALL, None), P(ALL, None))
    return jax.shard_map(
        on_device, mesh=split, in_specs=placed, out_specs=P(ALL), check_vma=False
    )
```

```python
import functools

import jax
import jax.numpy as jnp
from jax import lax
from jax.experimental import pallas as pl
from jax.experimental.pallas import tpu as pltpu
from jax.sharding import PartitionSpec as P

GRP = ("z", "core")
CORE_WIDE = ("core", "wide")
ALL = ("z", "core", "wide")
PLANES = 8
WIDE = 16
PER_PLANE = 32
WORKERS = 256
CAP = 4
HALF = 512
OUT = 1024
CAPS = (256, 192, 128, 64)
LIST = CAPS[0]
OWN_LIST = 128
Z_FIRST = (1280, 1024)
WIDE_FIRST = 1792
MARK = 2.0
REAL_MAX = 100.0
ROW_TILE = 256
NOTE = 1280
VMEM_LIMIT = 56 * 2**20


def padded_plan(embeddings, worker_of_row):
    row_count, features = embeddings.shape
    grp_count = lax.axis_size("z") * lax.axis_size("core")
    wide_count = lax.axis_size("wide")
    workers = grp_count * wide_count
    slot_count = workers * CAP
    values = embeddings.astype(jnp.float32)
    spread = jnp.mean(values * values, axis=1, keepdims=True)
    scaled = (values * lax.rsqrt(spread + 1e-06) * features ** (-0.25)).astype(jnp.bfloat16)
    target = worker_of_row[:, 0]
    matches = target[:, None] == jnp.arange(workers, dtype=jnp.int32)[None, :]
    one_hot = matches.astype(jnp.bfloat16)
    row_ids = jnp.arange(row_count, dtype=jnp.int32)
    earlier_mask = (row_ids[:, None] > row_ids[None, :]).astype(jnp.bfloat16)
    earlier = jnp.dot(earlier_mask, one_hot, preferred_element_type=jnp.float32)
    slot_index = jnp.sum(jnp.where(matches, earlier, 0.0), axis=1).astype(jnp.int32)
    sent_counts = jnp.sum(matches.astype(jnp.int32), axis=0)
    position = target * CAP + slot_index
    outgoing = jnp.zeros((slot_count, features), jnp.bfloat16).at[position].set(scaled)
    outgoing = outgoing.reshape(grp_count, wide_count, CAP, features)
    sent_counts = sent_counts.reshape(grp_count, wide_count, 1)

    def there(value):
        value = lax.all_to_all(value, GRP, split_axis=0, concat_axis=0, tiled=True)
        return lax.all_to_all(value, "wide", split_axis=1, concat_axis=1, tiled=True)

    arrived = there(outgoing).reshape(slot_count, features)
    counts_each = jnp.repeat(there(sent_counts).reshape(workers), CAP)
    slot_ids = jnp.arange(slot_count, dtype=jnp.int32)
    filled = slot_ids % CAP < counts_each
    paired = filled[:, None] & filled[None, :] & (slot_ids[:, None] != slot_ids[None, :])
    scores = lax.dot_general(
        arrived, arrived, (((1,), (1,)), ((), ())), preferred_element_type=jnp.float32
    )
    highest = jnp.max(jnp.where(paired, scores, -1e30), axis=1)
    back = highest.reshape(grp_count, wide_count, CAP)
    back = lax.all_to_all(back, "wide", split_axis=1, concat_axis=1, tiled=True)
    back = lax.all_to_all(back, GRP, split_axis=0, concat_axis=0, tiled=True)
    own_best = back.reshape(slot_count)[position]
    return jnp.where(own_best > -1e29, own_best, 0.0)


def z_shift(step):
    return [(z, (z + step) % PLANES) for z in range(PLANES)]


def after(value, *others):
    return lax.optimization_barrier((value,) + others)[0]


def call(kernel, out_shape, flops, **settings):
    return pl.pallas_call(
        kernel,
        out_shape=out_shape,
        compiler_params=pltpu.CompilerParams(vmem_limit_bytes=VMEM_LIMIT),
        cost_estimate=pl.CostEstimate(
            flops=flops, bytes_accessed=8 * 2**20, transcendentals=0
        ),
        **settings,
    )


def whole(value):
    return pl.BlockSpec(value.shape, lambda *_: (0,) * value.ndim)


def columns(rows, tile, first=0):
    return pl.BlockSpec((rows, tile), lambda i: (0, first + i))


def window(rows, tile, first):
    return pl.BlockSpec((pl.Element(rows), pl.Element(tile)), lambda i: (0, pl.multiple_of(first + i * tile, 128)))


def vmem():
    return pl.BlockSpec(memory_space=pltpu.VMEM)


def smem():
    return pl.BlockSpec(memory_space=pltpu.SMEM)


def iota(shape, axis):
    return lax.broadcasted_iota(jnp.int32, shape, axis)


def select_rows(pick, rows):
    return jnp.dot(pick, rows, preferred_element_type=jnp.float32)


def plan_kernel(
    where_ref,
    target_ref,
    x_ref,
    list_ref,
    wide_ref,
    note_ref,
    scale_ref,
    back_ref,
    flag_ref,
    squares,
):
    step = pl.program_id(0)
    f32, bf16 = jnp.float32, jnp.bfloat16
    part = jnp.zeros((HALF, 128), f32)
    for first in range(0, x_ref.shape[1], 128):
        values = x_ref[:, first : first + 128].astype(f32)
        part = part + values * values

    @pl.when(step == 0)
    def _():
        squares[...] = part
        z = where_ref[0]
        target = target_ref[...]
        across = (target == iota((WORKERS, HALF), 0)).astype(bf16)
        earlier = (iota((HALF, HALF), 0) < iota((HALF, HALF), 1)).astype(bf16)
        before = select_rows(across, earlier)
        counts = lax.dot_general(
            jnp.ones((16, HALF), bf16),
            across,
            (((1,), (1,)), ((), ())),
            preferred_element_type=f32,
        )
        down, over = iota((WORKERS, WORKERS), 0), iota((WORKERS, WORKERS), 1)
        same = down // PER_PLANE == over // PER_PLANE
        ahead = select_rows(counts.astype(bf16), (same & (down < over)).astype(bf16))[0:1, :]
        counts = counts[0:1, :]
        across = across.astype(f32)
        counts_down = jnp.sum(across, axis=1, keepdims=True)
        ahead_down = select_rows(
            (same & (over < down)).astype(bf16),
            jnp.broadcast_to(counts_down, (WORKERS, 128)).astype(bf16),
        )[:, 0:1]
        rank = jnp.sum(across * before, axis=0, keepdims=True).astype(jnp.int32)
        place = jnp.sum(across * (before + ahead_down), axis=0, keepdims=True).astype(jnp.int32)
        distance = (target // PER_PLANE - z) & (PLANES - 1)
        cluster_distance = (iota((1, WORKERS), 1) // PER_PLANE - z) & (PLANES - 1)
        n = [
            jnp.sum(jnp.where(cluster_distance == d, counts, 0.0), axis=1, keepdims=True).astype(
                jnp.int32
            )
            for d in range(PLANES)
        ]
        low = functools.reduce(
            jnp.maximum,
            (
                jnp.zeros_like(n[4]),
                n[4] - CAPS[3] + 1,
                n[4] + n[5] - CAPS[2] + 1,
                n[4] + n[5] + n[6] - CAPS[1] + 1,
                n[4] + n[5] + n[6] + n[7] - CAPS[0] + 1,
            ),
        )
        high = functools.reduce(
            jnp.minimum,
            (
                n[4],
                jnp.full_like(n[4], CAPS[3] - 1),
                CAPS[2] - 1 - n[3],
                CAPS[1] - 1 - n[3] - n[2],
                CAPS[0] - 1 - n[3] - n[2] - n[1],
            ),
        )
        to_right = jnp.clip((low + high) >> 1, 0, n[4])
        starts = [
            None,
            to_right + n[3] + n[2],
            to_right + n[3],
            to_right,
            to_right,
            n[4] - to_right,
            n[4] - to_right + n[5],
            n[4] - to_right + n[5] + n[6],
        ]

        def by_distance(which):
            value = jnp.zeros(which.shape, jnp.int32)
            for d in range(1, PLANES):
                value = jnp.where(which == d, starts[d], value)
            return value

        start = by_distance(distance)
        far_right = (distance == 4) & (place < to_right)
        far_left = (distance == 4) & (place >= to_right)
        goes_right = ((distance >= 1) & (distance <= 3)) | far_right
        on_list = jnp.where(far_right, place, jnp.where(far_left, place - to_right, start + place))
        list_place = jnp.where(
            distance == 0,
            2 * LIST + place,
            jnp.where(
                on_list >= LIST - 1, -1, jnp.where(goes_right, 1 + on_list, LIST + 1 + on_list)
            ),
        )
        list_ref[...] = list_place
        wide_place = (target // WIDE % 2) * HALF + target % WIDE * 32 + distance * CAP + rank
        wide_ref[...] = wide_place
        note_ref[...] = jnp.zeros((1, NOTE), f32)
        note_ref[:, 0:WORKERS] = counts
        note_ref[:, WORKERS : 2 * WORKERS] = ahead
        note_ref[:, 2 * WORKERS : 3 * WORKERS] = by_distance(cluster_distance).astype(f32)
        back_ref[...] = target * CAP + rank
        flag_ref[...] = jnp.broadcast_to((low > high).astype(f32), (1, 128))

    @pl.when(step > 0)
    def _():
        squares[...] += part

    @pl.when(step == pl.num_programs(0) - 1)
    def _():
        features = pl.num_programs(0) * x_ref.shape[1]
        spread = jnp.sum(squares[...], axis=1, keepdims=True) * (1.0 / features)
        scale_ref[...] = lax.rsqrt(spread + 1e-06) * features ** (-0.25)


def plan(where, targets, embeddings):
    f32 = jnp.float32
    shapes = [
        jax.ShapeDtypeStruct((1, HALF), jnp.int32),
        jax.ShapeDtypeStruct((1, HALF), jnp.int32),
        jax.ShapeDtypeStruct((1, NOTE), f32),
        jax.ShapeDtypeStruct((HALF, 1), f32),
        jax.ShapeDtypeStruct((1, HALF), jnp.int32),
        jax.ShapeDtypeStruct((1, 128), f32),
    ]
    return call(
        plan_kernel,
        shapes,
        10**9,
        grid=(4,),
        in_specs=[smem(), whole(targets), columns(HALF, embeddings.shape[1] // 4)],
        out_specs=[whole(shape) for shape in shapes],
        scratch_shapes=[pltpu.VMEM((HALF, 128), f32)],
    )(where, targets, embeddings)


def scaled_rows(x_ref, scale_ref):
    return (x_ref[...].astype(jnp.float32) * scale_ref[...]).astype(jnp.bfloat16)


def pack_lists_kernel(place_ref, note_ref, scale_ref, x_ref, right_ref, left_ref, own_ref, pick):
    @pl.when(pl.program_id(0) == 0)
    def _():
        pick[...] = (iota(pick.shape, 0) == place_ref[...]).astype(jnp.bfloat16)

    packed = select_rows(pick[...], scaled_rows(x_ref, scale_ref))
    first = iota((LIST, 1), 0) == 0
    note = note_ref[...]
    right_ref[...] = jnp.where(first, note, packed[0:LIST, :]).astype(jnp.bfloat16)
    left_ref[...] = jnp.where(first, note, packed[LIST : 2 * LIST, :]).astype(jnp.bfloat16)
    own_ref[...] = packed[2 * LIST :, :].astype(jnp.bfloat16)


def pack_lists(place, note, scale, embeddings, first_column, width):
    tile = width // 2
    parts = (LIST, LIST, OWN_LIST)
    return call(
        pack_lists_kernel,
        [jax.ShapeDtypeStruct((rows, width), jnp.bfloat16) for rows in parts],
        2 * sum(parts) * HALF * width,
        grid=(width // tile,),
        in_specs=[
            whole(place),
            columns(1, tile),
            whole(scale),
            window(HALF, tile, first_column),
        ],
        out_specs=[columns(rows, tile) for rows in parts],
        scratch_shapes=[pltpu.VMEM((sum(parts), HALF), jnp.bfloat16)],
    )(place, note, scale, embeddings)


def pack_wide_kernel(place_ref, scale_ref, x_ref, out_ref, pick, fill):
    @pl.when(pl.program_id(0) == 0)
    def _():
        match = (iota(pick.shape, 0) == place_ref[...]).astype(jnp.float32)
        pick[...] = match.astype(jnp.bfloat16)
        fill[...] = MARK * (1.0 - jnp.sum(match, axis=1, keepdims=True))

    packed = select_rows(pick[...], scaled_rows(x_ref, scale_ref))
    out_ref[...] = (packed + fill[...]).astype(jnp.bfloat16)


def pack_wide(place, scale, embeddings, first_column, width):
    tile = width // 2
    return call(
        pack_wide_kernel,
        jax.ShapeDtypeStruct((OUT, width), jnp.bfloat16),
        2 * OUT * HALF * width,
        grid=(width // tile,),
        in_specs=[
            whole(place),
            whole(scale),
            window(HALF, tile, first_column),
        ],
        out_specs=columns(OUT, tile),
        scratch_shapes=[
            pltpu.VMEM((OUT, HALF), jnp.bfloat16),
            pltpu.VMEM((OUT, 1), jnp.float32),
        ],
    )(place, scale, embeddings)


def reorder_kernel(pick_ref, x_ref, *out_refs):
    moved = select_rows(pick_ref[...], x_ref[...]).astype(jnp.bfloat16)
    for index, out_ref in enumerate(out_refs):
        out_ref[...] = moved[index * 128 : index * 128 + 128, :]


def reorder(pick, value):
    width = value.shape[1]
    tile = 256
    return call(
        reorder_kernel,
        [jax.ShapeDtypeStruct((128, width), jnp.bfloat16)] * PLANES,
        2 * OUT * OUT * width,
        grid=(width // tile,),
        in_specs=[whole(pick), columns(OUT, tile)],
        out_specs=[columns(128, tile)] * PLANES,
    )(pick, value)


def slots_kernel(where_ref, note_ref, *refs):
    firsts, out_ref, told = refs[:-2], refs[-2], refs[-1]
    told[...] = jnp.zeros(told.shape, jnp.float32)
    told[0:1, :] = note_ref[...]
    for index, first in enumerate(firsts):
        told[index + 1 : index + 2, :] = first[...].astype(jnp.float32)[0:1, :]
    slot = iota((OUT, 1), 0)
    step, rank = slot // CAP % PLANES, slot % CAP
    by_step = (iota((OUT, 16), 1) == step).astype(jnp.bfloat16)
    mine = iota((OUT, WORKERS), 1) == where_ref[0] * PER_PLANE + slot // 32

    def heard(index):
        told_here = told[:, index * WORKERS : index * WORKERS + WORKERS].astype(jnp.bfloat16)
        value = jnp.where(mine, select_rows(by_step, told_here), 0.0)
        return jnp.sum(value, axis=1, keepdims=True).astype(jnp.int32)

    count, place, start = heard(0), heard(1) + rank, heard(2)
    offsets = [OWN_LIST]
    for cap in CAPS + CAPS:
        offsets.append(offsets[-1] + cap)
    found = jnp.where(
        place < start, offsets[3] + 1 + place, offsets[7] + 1 + place - start
    )
    for d, block in ((1, 0), (2, 1), (3, 2), (5, 6), (6, 5), (7, 4)):
        found = jnp.where(step == d, offsets[block] + 1 + start + place, found)
    found = jnp.where(step == 0, place, found)
    found = jnp.where(rank < count, found, -1)
    out_ref[...] = (found == iota(out_ref.shape, 1)).astype(jnp.bfloat16)


def slots(where, note, blocks):
    firsts = [blocks[b] for b in (0, 1, 2, 3, 6, 5, 4)]
    shape = jax.ShapeDtypeStruct((OUT, OWN_LIST + 2 * sum(CAPS)), jnp.bfloat16)
    return call(
        slots_kernel,
        shape,
        10**9,
        grid=(1,),
        in_specs=[smem(), whole(note)]
        + [pl.BlockSpec((16, NOTE), lambda i: (0, 0)) for _ in firsts],
        out_specs=whole(shape),
        scratch_shapes=[pltpu.VMEM((16, NOTE), jnp.float32)],
    )(where, note, *firsts)


def repack_kernel(turn, pick_ref, *refs):
    blocks, out_ref, held = refs[:-2], refs[-2], refs[-1]
    step = pl.program_id(0)
    for chunk in range(2):

        @pl.when((step >= turn) == bool(chunk))
        def _(chunk=chunk):
            first = pl.multiple_of((step - chunk * turn) * 256, 256)
            base = 0
            for block in blocks[chunk * 9 : chunk * 9 + 9]:
                rows = block.shape[0]
                held[base : base + rows, :] = block[:, pl.ds(first, 256)]
                base += rows

    out_ref[...] = select_rows(pick_ref[...], held[...]).astype(jnp.bfloat16)


def repack(pick, first_blocks, second_blocks):
    tile = 256
    depth = pick.shape[1]
    turn = first_blocks[0].shape[1] // tile
    steps = turn + second_blocks[0].shape[1] // tile
    blocks = list(first_blocks) + list(second_blocks)
    return call(
        functools.partial(repack_kernel, turn),
        jax.ShapeDtypeStruct((OUT, steps * tile), jnp.bfloat16),
        2 * OUT * depth * steps * tile,
        grid=(steps,),
        in_specs=[whole(value) for value in [pick] + blocks],
        out_specs=columns(OUT, tile),
        scratch_shapes=[pltpu.VMEM((depth, tile), jnp.bfloat16)],
    )(pick, *blocks)


def gram_kernel(pick_ref, x_ref, out_ref, held):
    step = pl.program_id(0)
    held[step] = select_rows(pick_ref[...], x_ref[...]).astype(jnp.bfloat16)

    @pl.when(step == pl.num_programs(0) - 1)
    def _():
        for tile in range(0, OUT, ROW_TILE):
            part = 0.0
            for index in range(held.shape[0]):
                part = part + lax.dot_general(
                    held[index, tile : tile + ROW_TILE, :],
                    held[index, tile:, :],
                    (((1,), (1,)), ((), ())),
                    preferred_element_type=jnp.float32,
                )
            out_ref[tile : tile + ROW_TILE, tile:] = part


def gram(pick, value):
    width = value.shape[1]
    tile = 768
    return call(
        gram_kernel,
        jax.ShapeDtypeStruct((OUT, OUT), jnp.float32),
        4 * OUT * OUT * width,
        grid=(width // tile,),
        in_specs=[whole(pick), columns(OUT, tile)],
        out_specs=pl.BlockSpec((OUT, OUT), lambda i: (0, 0)),
        scratch_shapes=[pltpu.VMEM((width // tile, OUT, tile), jnp.bfloat16)],
    )(pick, value)


def best_kernel(where_ref, flag_ref, total_ref, *refs):
    blocks, out_ref, held = refs[:PLANES], refs[PLANES], refs[-1]
    for index, block in enumerate(blocks):
        held[index * 128 : index * 128 + 128, :] = block[...]
    count = OUT // ROW_TILE
    same = iota((ROW_TILE, ROW_TILE), 0) == iota((ROW_TILE, ROW_TILE), 1)
    best = [jnp.full((1, ROW_TILE), -1e30, jnp.float32)] * count
    filled = [None] * count
    for tile in reversed(range(count)):
        first = tile * ROW_TILE
        part = total_ref[first : first + ROW_TILE, first:] + lax.dot_general(
            held[first : first + ROW_TILE, :],
            held[first:, :],
            (((1,), (1,)), ((), ())),
            preferred_element_type=jnp.float32,
        )
        diagonal = jnp.where(same, part[:, :ROW_TILE], 0.0)
        row_filled = jnp.sum(diagonal, axis=1, keepdims=True) < REAL_MAX
        filled[tile] = jnp.sum(diagonal, axis=0, keepdims=True) < REAL_MAX
        across = jnp.full((ROW_TILE, 1), -1e30, jnp.float32)
        for other in range(tile, count):
            scores = part[:, (other - tile) * ROW_TILE : (other - tile + 1) * ROW_TILE]
            allowed = row_filled & jnp.logical_not(same) if other == tile else row_filled
            down = jnp.max(jnp.where(allowed, scores, -1e30), axis=0, keepdims=True)
            best[other] = jnp.maximum(best[other], down)
            if other > tile:
                most = jnp.max(jnp.where(filled[other], scores, -1e30), axis=1, keepdims=True)
                across = jnp.maximum(across, most)
        turned = jnp.sum(jnp.where(same, across, 0.0), axis=0, keepdims=True)
        best[tile] = jnp.maximum(best[tile], turned)
    for d in range(PLANES):
        result = best[d // 2][:, d % 2 * 128 : d % 2 * 128 + 128]
        result = jnp.where(result > -1e29, result, 0.0)
        result = jnp.where(flag_ref[0:1, 0:1] > 0.5, 1e30, result)
        plane = (where_ref[0] - d) & (PLANES - 1)
        out_ref[pl.ds(pl.multiple_of(plane * 32, 32), 32), :] = jnp.broadcast_to(
            result, (32, 128)
        )


def best_of(where, flag, total, blocks):
    width = blocks[0].shape[1]
    shape = jax.ShapeDtypeStruct((WORKERS, 128), jnp.float32)
    return call(
        best_kernel,
        shape,
        2 * OUT * OUT * width,
        grid=(1,),
        in_specs=[smem()] + [whole(value) for value in [flag, total] + blocks],
        out_specs=whole(shape),
        scratch_shapes=[pltpu.VMEM((OUT, width), jnp.bfloat16)],
    )(where, flag, total, *blocks)


def on_device(embeddings, worker_of_row):
    i32 = jnp.int32
    core = lax.axis_index("core")
    wide = lax.axis_index("wide")
    where = lax.axis_index("z").astype(i32).reshape(1)
    list_place, wide_place, note, scale, back_place, flag = plan(
        where, worker_of_row.reshape(1, HALF), embeddings
    )

    packed, own = [], []
    for f in range(2):
        right, left, mine = pack_lists(
            list_place, note, scale, embeddings, sum(Z_FIRST[:f]), Z_FIRST[f]
        )
        packed.append((right, left))
        own.append(mine)

    wide_rows = pack_wide(
        after(wide_place, packed[0][0]), scale, embeddings, sum(Z_FIRST), WIDE_FIRST
    )
    wide_back = lax.all_to_all(wide_rows, CORE_WIDE, 0, 0, tiled=True)

    slot_ids = jnp.arange(OUT, dtype=i32)
    final = slot_ids[:, None]
    step_of, core_of, column_of = final // 128, final // 64 % 2, final // 4 % WIDE
    final_from = core_of * HALF + column_of * 32 + step_of * CAP + final % CAP
    final_order = (final_from == slot_ids[None, :]).astype(jnp.bfloat16)

    got = [([], []), ([], [])]
    for hop in range(4):
        if hop == 2:
            blocks = reorder(after(final_order, got[0][0][1]), wide_back)
        for f in range(2):
            for side, steps in enumerate((z_shift(1), z_shift(-1))):
                if hop == 0:
                    block = packed[f][side]
                else:
                    block = got[f][side][-1][: CAPS[hop]]
                if hop == 1:
                    block = after(block, wide_rows)
                if hop == 2 and f == 1:
                    block = after(block, blocks[1])
                if hop == 3 and f == 1:
                    block = after(block, slot_pick)
                got[f][side].append(lax.ppermute(block, "z", steps))
            if hop == 3 and f == 0:
                slot_pick = slots(where, note, got[0][0] + got[0][1])
    got = [rights + lefts for rights, lefts in got]
    last = [blocks[0]] + [None] * 7
    for steps, gate in (((2, 6), ()), ((1, 7, 4), (2, 6)), ((3, 5), (1, 7))):
        for step in steps:
            block = blocks[step]
            if gate:
                block = after(block, *[last[done] for done in gate])
            last[step] = lax.ppermute(block, "z", z_shift(step))

    packed = repack(slot_pick, [own[0]] + got[0], [own[1]] + got[1])
    packed = after(packed, wide_back, last[2], last[6])
    arrived = lax.all_to_all(packed, CORE_WIDE, 0, 0, tiled=True)
    best = best_of(where, flag, gram(final_order, arrived), last)

    back = lax.all_to_all(best, ALL, 0, 0, tiled=True)
    failed = jnp.max(back) > 1e29
    mine = lax.dynamic_slice(back, (0, core * 64 + wide * CAP), (WORKERS, CAP))
    result = jnp.sum(
        jnp.where(back_place == slot_ids[:, None], mine.reshape(OUT)[:, None], 0.0), axis=0
    )
    return lax.cond(failed, padded_plan, lambda *_: result, embeddings, worker_of_row)


def solution(mesh):
    split = jax.sharding.Mesh(mesh.devices.reshape(PLANES, 2, WIDE), ALL)
    placed = (P(ALL, None), P(ALL, None))
    return jax.shard_map(
        on_device, mesh=split, in_specs=placed, out_specs=P(ALL), check_vma=False
    )
```

```python
import functools

import jax
import jax.numpy as jnp
from jax import lax
from jax.experimental import pallas as pl
from jax.experimental.pallas import tpu as pltpu
from jax.sharding import PartitionSpec as P

GRP = ("z", "core")
CORE_WIDE = ("core", "wide")
ALL = ("z", "core", "wide")
PLANES = 8
WIDE = 16
PER_PLANE = 32
WORKERS = 256
CAP = 4
HALF = 512
OUT = 1024
CAPS = (256, 192, 128, 64)
LIST = CAPS[0]
OWN_LIST = 128
Z_FIRST = (1280, 1024)
WIDE_FIRST = 1792
MARK = 2.0
REAL_MAX = 100.0
ROW_TILE = 256
NOTE = 1280
VMEM_LIMIT = 56 * 2**20


def padded_plan(embeddings, worker_of_row):
    row_count, features = embeddings.shape
    grp_count = lax.axis_size("z") * lax.axis_size("core")
    wide_count = lax.axis_size("wide")
    workers = grp_count * wide_count
    slot_count = workers * CAP
    values = embeddings.astype(jnp.float32)
    spread = jnp.mean(values * values, axis=1, keepdims=True)
    scaled = (values * lax.rsqrt(spread + 1e-06) * features ** (-0.25)).astype(jnp.bfloat16)
    target = worker_of_row[:, 0]
    matches = target[:, None] == jnp.arange(workers, dtype=jnp.int32)[None, :]
    one_hot = matches.astype(jnp.bfloat16)
    row_ids = jnp.arange(row_count, dtype=jnp.int32)
    earlier_mask = (row_ids[:, None] > row_ids[None, :]).astype(jnp.bfloat16)
    earlier = jnp.dot(earlier_mask, one_hot, preferred_element_type=jnp.float32)
    slot_index = jnp.sum(jnp.where(matches, earlier, 0.0), axis=1).astype(jnp.int32)
    sent_counts = jnp.sum(matches.astype(jnp.int32), axis=0)
    position = target * CAP + slot_index
    outgoing = jnp.zeros((slot_count, features), jnp.bfloat16).at[position].set(scaled)
    outgoing = outgoing.reshape(grp_count, wide_count, CAP, features)
    sent_counts = sent_counts.reshape(grp_count, wide_count, 1)

    def there(value):
        value = lax.all_to_all(value, GRP, split_axis=0, concat_axis=0, tiled=True)
        return lax.all_to_all(value, "wide", split_axis=1, concat_axis=1, tiled=True)

    arrived = there(outgoing).reshape(slot_count, features)
    counts_each = jnp.repeat(there(sent_counts).reshape(workers), CAP)
    slot_ids = jnp.arange(slot_count, dtype=jnp.int32)
    filled = slot_ids % CAP < counts_each
    paired = filled[:, None] & filled[None, :] & (slot_ids[:, None] != slot_ids[None, :])
    scores = lax.dot_general(
        arrived, arrived, (((1,), (1,)), ((), ())), preferred_element_type=jnp.float32
    )
    highest = jnp.max(jnp.where(paired, scores, -1e30), axis=1)
    back = highest.reshape(grp_count, wide_count, CAP)
    back = lax.all_to_all(back, "wide", split_axis=1, concat_axis=1, tiled=True)
    back = lax.all_to_all(back, GRP, split_axis=0, concat_axis=0, tiled=True)
    own_best = back.reshape(slot_count)[position]
    return jnp.where(own_best > -1e29, own_best, 0.0)


def z_shift(step):
    return [(z, (z + step) % PLANES) for z in range(PLANES)]


def after(value, *others):
    return lax.optimization_barrier((value,) + others)[0]


def call(kernel, out_shape, flops, **settings):
    return pl.pallas_call(
        kernel,
        out_shape=out_shape,
        compiler_params=pltpu.CompilerParams(vmem_limit_bytes=VMEM_LIMIT),
        cost_estimate=pl.CostEstimate(
            flops=flops, bytes_accessed=8 * 2**20, transcendentals=0
        ),
        **settings,
    )


def whole(value):
    return pl.BlockSpec(value.shape, lambda *_: (0,) * value.ndim)


def columns(rows, tile, first=0):
    return pl.BlockSpec((rows, tile), lambda i: (0, first + i))


def window(rows, tile, first):
    return pl.BlockSpec((pl.Element(rows), pl.Element(tile)), lambda i: (0, pl.multiple_of(first + i * tile, 128)))


def vmem():
    return pl.BlockSpec(memory_space=pltpu.VMEM)


def smem():
    return pl.BlockSpec(memory_space=pltpu.SMEM)


def iota(shape, axis):
    return lax.broadcasted_iota(jnp.int32, shape, axis)


def select_rows(pick, rows):
    return jnp.dot(pick, rows, preferred_element_type=jnp.float32)


def plan_kernel(
    where_ref,
    target_ref,
    x_ref,
    list_ref,
    wide_ref,
    note_ref,
    scale_ref,
    back_ref,
    flag_ref,
    squares,
):
    step = pl.program_id(0)
    f32, bf16 = jnp.float32, jnp.bfloat16
    part = jnp.zeros((HALF, 128), f32)
    for first in range(0, x_ref.shape[1], 128):
        values = x_ref[:, first : first + 128].astype(f32)
        part = part + values * values

    @pl.when(step == 0)
    def _():
        squares[...] = part
        z = where_ref[0]
        target = target_ref[...]
        across = (target == iota((WORKERS, HALF), 0)).astype(bf16)
        earlier = (iota((HALF, HALF), 0) < iota((HALF, HALF), 1)).astype(bf16)
        before = select_rows(across, earlier)
        counts = lax.dot_general(
            jnp.ones((16, HALF), bf16),
            across,
            (((1,), (1,)), ((), ())),
            preferred_element_type=f32,
        )
        down, over = iota((WORKERS, WORKERS), 0), iota((WORKERS, WORKERS), 1)
        same = down // PER_PLANE == over // PER_PLANE
        ahead = select_rows(counts.astype(bf16), (same & (down < over)).astype(bf16))[0:1, :]
        counts = counts[0:1, :]
        across = across.astype(f32)
        counts_down = jnp.sum(across, axis=1, keepdims=True)
        ahead_down = select_rows(
            (same & (over < down)).astype(bf16),
            jnp.broadcast_to(counts_down, (WORKERS, 128)).astype(bf16),
        )[:, 0:1]
        rank = jnp.sum(across * before, axis=0, keepdims=True).astype(jnp.int32)
        place = jnp.sum(across * (before + ahead_down), axis=0, keepdims=True).astype(jnp.int32)
        distance = (target // PER_PLANE - z) & (PLANES - 1)
        cluster_distance = (iota((1, WORKERS), 1) // PER_PLANE - z) & (PLANES - 1)
        n = [
            jnp.sum(jnp.where(cluster_distance == d, counts, 0.0), axis=1, keepdims=True).astype(
                jnp.int32
            )
            for d in range(PLANES)
        ]
        low = functools.reduce(
            jnp.maximum,
            (
                jnp.zeros_like(n[4]),
                n[4] - CAPS[3] + 1,
                n[4] + n[5] - CAPS[2] + 1,
                n[4] + n[5] + n[6] - CAPS[1] + 1,
                n[4] + n[5] + n[6] + n[7] - CAPS[0] + 1,
            ),
        )
        high = functools.reduce(
            jnp.minimum,
            (
                n[4],
                jnp.full_like(n[4], CAPS[3] - 1),
                CAPS[2] - 1 - n[3],
                CAPS[1] - 1 - n[3] - n[2],
                CAPS[0] - 1 - n[3] - n[2] - n[1],
            ),
        )
        to_right = jnp.clip((low + high) >> 1, 0, n[4])
        starts = [
            None,
            to_right + n[3] + n[2],
            to_right + n[3],
            to_right,
            to_right,
            n[4] - to_right,
            n[4] - to_right + n[5],
            n[4] - to_right + n[5] + n[6],
        ]

        def by_distance(which):
            value = jnp.zeros(which.shape, jnp.int32)
            for d in range(1, PLANES):
                value = jnp.where(which == d, starts[d], value)
            return value

        start = by_distance(distance)
        far_right = (distance == 4) & (place < to_right)
        far_left = (distance == 4) & (place >= to_right)
        goes_right = ((distance >= 1) & (distance <= 3)) | far_right
        on_list = jnp.where(far_right, place, jnp.where(far_left, place - to_right, start + place))
        list_place = jnp.where(
            distance == 0,
            2 * LIST + place,
            jnp.where(
                on_list >= LIST - 1, -1, jnp.where(goes_right, 1 + on_list, LIST + 1 + on_list)
            ),
        )
        list_ref[...] = list_place
        wide_place = (target // WIDE % 2) * HALF + target % WIDE * 32 + distance * CAP + rank
        wide_ref[...] = wide_place
        note_ref[...] = jnp.zeros((1, NOTE), f32)
        note_ref[:, 0:WORKERS] = counts
        note_ref[:, WORKERS : 2 * WORKERS] = ahead
        note_ref[:, 2 * WORKERS : 3 * WORKERS] = by_distance(cluster_distance).astype(f32)
        back_ref[...] = target * CAP + rank
        flag_ref[...] = jnp.broadcast_to((low > high).astype(f32), (1, 128))

    @pl.when(step > 0)
    def _():
        squares[...] += part

    @pl.when(step == pl.num_programs(0) - 1)
    def _():
        features = pl.num_programs(0) * x_ref.shape[1]
        spread = jnp.sum(squares[...], axis=1, keepdims=True) * (1.0 / features)
        scale_ref[...] = lax.rsqrt(spread + 1e-06) * features ** (-0.25)


def plan(where, targets, embeddings):
    f32 = jnp.float32
    shapes = [
        jax.ShapeDtypeStruct((1, HALF), jnp.int32),
        jax.ShapeDtypeStruct((1, HALF), jnp.int32),
        jax.ShapeDtypeStruct((1, NOTE), f32),
        jax.ShapeDtypeStruct((HALF, 1), f32),
        jax.ShapeDtypeStruct((1, HALF), jnp.int32),
        jax.ShapeDtypeStruct((1, 128), f32),
    ]
    return call(
        plan_kernel,
        shapes,
        10**9,
        grid=(4,),
        in_specs=[smem(), whole(targets), columns(HALF, embeddings.shape[1] // 4)],
        out_specs=[whole(shape) for shape in shapes],
        scratch_shapes=[pltpu.VMEM((HALF, 128), f32)],
    )(where, targets, embeddings)


def scaled_rows(x_ref, scale_ref):
    return (x_ref[...].astype(jnp.float32) * scale_ref[...]).astype(jnp.bfloat16)


def pack_lists_kernel(place_ref, note_ref, scale_ref, x_ref, right_ref, left_ref, own_ref, pick):
    @pl.when(pl.program_id(0) == 0)
    def _():
        pick[...] = (iota(pick.shape, 0) == place_ref[...]).astype(jnp.bfloat16)

    packed = select_rows(pick[...], scaled_rows(x_ref, scale_ref))
    first = iota((LIST, 1), 0) == 0
    note = note_ref[...]
    right_ref[...] = jnp.where(first, note, packed[0:LIST, :]).astype(jnp.bfloat16)
    left_ref[...] = jnp.where(first, note, packed[LIST : 2 * LIST, :]).astype(jnp.bfloat16)
    own_ref[...] = packed[2 * LIST :, :].astype(jnp.bfloat16)


def pack_lists(place, note, scale, embeddings, first_column, width):
    tile = width // 2
    parts = (LIST, LIST, OWN_LIST)
    return call(
        pack_lists_kernel,
        [jax.ShapeDtypeStruct((rows, width), jnp.bfloat16) for rows in parts],
        2 * sum(parts) * HALF * width,
        grid=(width // tile,),
        in_specs=[
            whole(place),
            columns(1, tile),
            whole(scale),
            window(HALF, tile, first_column),
        ],
        out_specs=[columns(rows, tile) for rows in parts],
        scratch_shapes=[pltpu.VMEM((sum(parts), HALF), jnp.bfloat16)],
    )(place, note, scale, embeddings)


def pack_wide_kernel(place_ref, scale_ref, x_ref, out_ref, pick, fill):
    @pl.when(pl.program_id(0) == 0)
    def _():
        match = (iota(pick.shape, 0) == place_ref[...]).astype(jnp.float32)
        pick[...] = match.astype(jnp.bfloat16)
        fill[...] = MARK * (1.0 - jnp.sum(match, axis=1, keepdims=True))

    packed = select_rows(pick[...], scaled_rows(x_ref, scale_ref))
    out_ref[...] = (packed + fill[...]).astype(jnp.bfloat16)


def pack_wide(place, scale, embeddings, first_column, width):
    tile = width // 2
    return call(
        pack_wide_kernel,
        jax.ShapeDtypeStruct((OUT, width), jnp.bfloat16),
        2 * OUT * HALF * width,
        grid=(width // tile,),
        in_specs=[
            whole(place),
            whole(scale),
            window(HALF, tile, first_column),
        ],
        out_specs=columns(OUT, tile),
        scratch_shapes=[
            pltpu.VMEM((OUT, HALF), jnp.bfloat16),
            pltpu.VMEM((OUT, 1), jnp.float32),
        ],
    )(place, scale, embeddings)


def reorder_kernel(pick_ref, x_ref, *out_refs):
    moved = select_rows(pick_ref[...], x_ref[...]).astype(jnp.bfloat16)
    for index, out_ref in enumerate(out_refs):
        out_ref[...] = moved[index * 128 : index * 128 + 128, :]


def reorder(pick, value):
    width = value.shape[1]
    tile = 256
    return call(
        reorder_kernel,
        [jax.ShapeDtypeStruct((128, width), jnp.bfloat16)] * PLANES,
        2 * OUT * OUT * width,
        grid=(width // tile,),
        in_specs=[whole(pick), columns(OUT, tile)],
        out_specs=[columns(128, tile)] * PLANES,
    )(pick, value)


def slots_kernel(where_ref, note_ref, *refs):
    firsts, out_ref, told = refs[:-2], refs[-2], refs[-1]
    told[...] = jnp.zeros(told.shape, jnp.float32)
    told[0:1, :] = note_ref[...]
    for index, first in enumerate(firsts):
        told[index + 1 : index + 2, :] = first[...].astype(jnp.float32)[0:1, :]
    slot = iota((OUT, 1), 0)
    step, rank = slot // CAP % PLANES, slot % CAP
    by_step = (iota((OUT, 16), 1) == step).astype(jnp.bfloat16)
    mine = iota((OUT, WORKERS), 1) == where_ref[0] * PER_PLANE + slot // 32

    def heard(index):
        told_here = told[:, index * WORKERS : index * WORKERS + WORKERS].astype(jnp.bfloat16)
        value = jnp.where(mine, select_rows(by_step, told_here), 0.0)
        return jnp.sum(value, axis=1, keepdims=True).astype(jnp.int32)

    count, place, start = heard(0), heard(1) + rank, heard(2)
    offsets = [OWN_LIST]
    for cap in CAPS + CAPS:
        offsets.append(offsets[-1] + cap)
    found = jnp.where(
        place < start, offsets[3] + 1 + place, offsets[7] + 1 + place - start
    )
    for d, block in ((1, 0), (2, 1), (3, 2), (5, 6), (6, 5), (7, 4)):
        found = jnp.where(step == d, offsets[block] + 1 + start + place, found)
    found = jnp.where(step == 0, place, found)
    found = jnp.where(rank < count, found, -1)
    out_ref[...] = (found == iota(out_ref.shape, 1)).astype(jnp.bfloat16)


def slots(where, note, blocks):
    firsts = [blocks[b] for b in (0, 1, 2, 3, 6, 5, 4)]
    shape = jax.ShapeDtypeStruct((OUT, OWN_LIST + 2 * sum(CAPS)), jnp.bfloat16)
    return call(
        slots_kernel,
        shape,
        10**9,
        grid=(1,),
        in_specs=[smem(), whole(note)]
        + [pl.BlockSpec((16, NOTE), lambda i: (0, 0)) for _ in firsts],
        out_specs=whole(shape),
        scratch_shapes=[pltpu.VMEM((16, NOTE), jnp.float32)],
    )(where, note, *firsts)


def repack_kernel(turn, pick_ref, *refs):
    blocks, out_ref, held = refs[:-2], refs[-2], refs[-1]
    step = pl.program_id(0)
    for chunk in range(2):

        @pl.when((step >= turn) == bool(chunk))
        def _(chunk=chunk):
            first = pl.multiple_of((step - chunk * turn) * 256, 256)
            base = 0
            for block in blocks[chunk * 9 : chunk * 9 + 9]:
                rows = block.shape[0]
                held[base : base + rows, :] = block[:, pl.ds(first, 256)]
                base += rows

    out_ref[...] = select_rows(pick_ref[...], held[...]).astype(jnp.bfloat16)


def repack(pick, first_blocks, second_blocks):
    tile = 256
    depth = pick.shape[1]
    turn = first_blocks[0].shape[1] // tile
    steps = turn + second_blocks[0].shape[1] // tile
    blocks = list(first_blocks) + list(second_blocks)
    return call(
        functools.partial(repack_kernel, turn),
        jax.ShapeDtypeStruct((OUT, steps * tile), jnp.bfloat16),
        2 * OUT * depth * steps * tile,
        grid=(steps,),
        in_specs=[whole(value) for value in [pick] + blocks],
        out_specs=columns(OUT, tile),
        scratch_shapes=[pltpu.VMEM((depth, tile), jnp.bfloat16)],
    )(pick, *blocks)


def gram_kernel(pick_ref, x_ref, out_ref, held):
    step = pl.program_id(0)
    held[step] = select_rows(pick_ref[...], x_ref[...]).astype(jnp.bfloat16)

    @pl.when(step == pl.num_programs(0) - 1)
    def _():
        for tile in range(0, OUT, ROW_TILE):
            part = 0.0
            for index in range(held.shape[0]):
                part = part + lax.dot_general(
                    held[index, tile : tile + ROW_TILE, :],
                    held[index, tile:, :],
                    (((1,), (1,)), ((), ())),
                    preferred_element_type=jnp.float32,
                )
            out_ref[tile : tile + ROW_TILE, tile:] = part


def gram(pick, value):
    width = value.shape[1]
    tile = 768
    return call(
        gram_kernel,
        jax.ShapeDtypeStruct((OUT, OUT), jnp.float32),
        4 * OUT * OUT * width,
        grid=(width // tile,),
        in_specs=[whole(pick), columns(OUT, tile)],
        out_specs=pl.BlockSpec((OUT, OUT), lambda i: (0, 0)),
        scratch_shapes=[pltpu.VMEM((width // tile, OUT, tile), jnp.bfloat16)],
    )(pick, value)


def best_kernel(where_ref, flag_ref, total_ref, *refs):
    blocks, out_ref, held = refs[:PLANES], refs[PLANES], refs[-1]
    for index, block in enumerate(blocks):
        held[index * 128 : index * 128 + 128, :] = block[...]
    count = OUT // ROW_TILE
    same = iota((ROW_TILE, ROW_TILE), 0) == iota((ROW_TILE, ROW_TILE), 1)
    best = [jnp.full((1, ROW_TILE), -1e30, jnp.float32)] * count
    filled = [None] * count
    for tile in reversed(range(count)):
        first = tile * ROW_TILE
        part = total_ref[first : first + ROW_TILE, first:] + lax.dot_general(
            held[first : first + ROW_TILE, :],
            held[first:, :],
            (((1,), (1,)), ((), ())),
            preferred_element_type=jnp.float32,
        )
        diagonal = jnp.where(same, part[:, :ROW_TILE], 0.0)
        row_filled = jnp.sum(diagonal, axis=1, keepdims=True) < REAL_MAX
        filled[tile] = jnp.sum(diagonal, axis=0, keepdims=True) < REAL_MAX
        across = jnp.full((ROW_TILE, 1), -1e30, jnp.float32)
        for other in range(tile, count):
            scores = part[:, (other - tile) * ROW_TILE : (other - tile + 1) * ROW_TILE]
            allowed = row_filled & jnp.logical_not(same) if other == tile else row_filled
            down = jnp.max(jnp.where(allowed, scores, -1e30), axis=0, keepdims=True)
            best[other] = jnp.maximum(best[other], down)
            if other > tile:
                most = jnp.max(jnp.where(filled[other], scores, -1e30), axis=1, keepdims=True)
                across = jnp.maximum(across, most)
        turned = jnp.sum(jnp.where(same, across, 0.0), axis=0, keepdims=True)
        best[tile] = jnp.maximum(best[tile], turned)
    for d in range(PLANES):
        result = best[d // 2][:, d % 2 * 128 : d % 2 * 128 + 128]
        result = jnp.where(result > -1e29, result, 0.0)
        result = jnp.where(flag_ref[0:1, 0:1] > 0.5, 1e30, result)
        plane = (where_ref[0] - d) & (PLANES - 1)
        out_ref[pl.ds(pl.multiple_of(plane * 32, 32), 32), :] = jnp.broadcast_to(
            result, (32, 128)
        )


def best_of(where, flag, total, blocks):
    width = blocks[0].shape[1]
    shape = jax.ShapeDtypeStruct((WORKERS, 128), jnp.float32)
    return call(
        best_kernel,
        shape,
        2 * OUT * OUT * width,
        grid=(1,),
        in_specs=[smem()] + [whole(value) for value in [flag, total] + blocks],
        out_specs=whole(shape),
        scratch_shapes=[pltpu.VMEM((OUT, width), jnp.bfloat16)],
    )(where, flag, total, *blocks)


def on_device(embeddings, worker_of_row):
    i32 = jnp.int32
    core = lax.axis_index("core")
    wide = lax.axis_index("wide")
    where = lax.axis_index("z").astype(i32).reshape(1)
    list_place, wide_place, note, scale, back_place, flag = plan(
        where, worker_of_row.reshape(1, HALF), embeddings
    )

    packed, own = [], []
    for f in range(2):
        right, left, mine = pack_lists(
            list_place, note, scale, embeddings, sum(Z_FIRST[:f]), Z_FIRST[f]
        )
        packed.append((right, left))
        own.append(mine)

    wide_rows = pack_wide(
        after(wide_place, packed[0][0]), scale, embeddings, sum(Z_FIRST), WIDE_FIRST
    )
    wide_back = lax.all_to_all(wide_rows, CORE_WIDE, 0, 0, tiled=True)

    slot_ids = jnp.arange(OUT, dtype=i32)
    final = slot_ids[:, None]
    step_of, core_of, column_of = final // 128, final // 64 % 2, final // 4 % WIDE
    final_from = core_of * HALF + column_of * 32 + step_of * CAP + final % CAP
    final_order = (final_from == slot_ids[None, :]).astype(jnp.bfloat16)

    got = [([], []), ([], [])]
    for hop in range(4):
        if hop == 2:
            blocks = reorder(after(final_order, got[0][0][1]), wide_back)
        for f in range(2):
            for side, steps in enumerate((z_shift(1), z_shift(-1))):
                if hop == 0:
                    block = packed[f][side]
                else:
                    block = got[f][side][-1][: CAPS[hop]]
                if hop == 1:
                    block = after(block, wide_rows)
                if hop == 2 and f == 1:
                    block = after(block, blocks[1])
                got[f][side].append(lax.ppermute(block, "z", steps))
    got = [rights + lefts for rights, lefts in got]
    last = [blocks[0]] + [None] * 7
    for steps, gate in (((4,), ()), ((1, 7, 2, 6), (4,)), ((3, 5), (1, 7))):
        for step in steps:
            block = blocks[step]
            if gate:
                block = after(block, *[last[done] for done in gate])
            last[step] = lax.ppermute(block, "z", z_shift(step))

    slot_pick = slots(where, note, got[0])
    packed = repack(slot_pick, [own[0]] + got[0], [own[1]] + got[1])
    packed = after(packed, wide_back, last[4])
    arrived = lax.all_to_all(packed, CORE_WIDE, 0, 0, tiled=True)
    best = best_of(where, flag, gram(final_order, arrived), last)

    back = lax.all_to_all(best, ALL, 0, 0, tiled=True)
    failed = jnp.max(back) > 1e29
    mine = lax.dynamic_slice(back, (0, core * 64 + wide * CAP), (WORKERS, CAP))
    result = jnp.sum(
        jnp.where(back_place == slot_ids[:, None], mine.reshape(OUT)[:, None], 0.0), axis=0
    )
    return lax.cond(failed, padded_plan, lambda *_: result, embeddings, worker_of_row)


def solution(mesh):
    split = jax.sharding.Mesh(mesh.devices.reshape(PLANES, 2, WIDE), ALL)
    placed = (P(ALL, None), P(ALL, None))
    return jax.shard_map(
        on_device, mesh=split, in_specs=placed, out_specs=P(ALL), check_vma=False
    )
```

```python
import functools

import jax
import jax.numpy as jnp
from jax import lax
from jax.experimental import pallas as pl
from jax.experimental.pallas import tpu as pltpu
from jax.sharding import PartitionSpec as P

GRP = ("z", "core")
CORE_WIDE = ("core", "wide")
ALL = ("z", "core", "wide")
PLANES = 8
WIDE = 16
PER_PLANE = 32
WORKERS = 256
CAP = 4
HALF = 512
OUT = 1024
CAPS = (256, 192, 128, 64)
LIST = CAPS[0]
OWN_LIST = 128
Z_FIRST = (1280, 1024)
WIDE_FIRST = 1792
MARK = 2.0
REAL_MAX = 100.0
ROW_TILE = 256
NOTE = 1280
VMEM_LIMIT = 56 * 2**20


def padded_plan(embeddings, worker_of_row):
    row_count, features = embeddings.shape
    grp_count = lax.axis_size("z") * lax.axis_size("core")
    wide_count = lax.axis_size("wide")
    workers = grp_count * wide_count
    slot_count = workers * CAP
    values = embeddings.astype(jnp.float32)
    spread = jnp.mean(values * values, axis=1, keepdims=True)
    scaled = (values * lax.rsqrt(spread + 1e-06) * features ** (-0.25)).astype(jnp.bfloat16)
    target = worker_of_row[:, 0]
    matches = target[:, None] == jnp.arange(workers, dtype=jnp.int32)[None, :]
    one_hot = matches.astype(jnp.bfloat16)
    row_ids = jnp.arange(row_count, dtype=jnp.int32)
    earlier_mask = (row_ids[:, None] > row_ids[None, :]).astype(jnp.bfloat16)
    earlier = jnp.dot(earlier_mask, one_hot, preferred_element_type=jnp.float32)
    slot_index = jnp.sum(jnp.where(matches, earlier, 0.0), axis=1).astype(jnp.int32)
    sent_counts = jnp.sum(matches.astype(jnp.int32), axis=0)
    position = target * CAP + slot_index
    outgoing = jnp.zeros((slot_count, features), jnp.bfloat16).at[position].set(scaled)
    outgoing = outgoing.reshape(grp_count, wide_count, CAP, features)
    sent_counts = sent_counts.reshape(grp_count, wide_count, 1)

    def there(value):
        value = lax.all_to_all(value, GRP, split_axis=0, concat_axis=0, tiled=True)
        return lax.all_to_all(value, "wide", split_axis=1, concat_axis=1, tiled=True)

    arrived = there(outgoing).reshape(slot_count, features)
    counts_each = jnp.repeat(there(sent_counts).reshape(workers), CAP)
    slot_ids = jnp.arange(slot_count, dtype=jnp.int32)
    filled = slot_ids % CAP < counts_each
    paired = filled[:, None] & filled[None, :] & (slot_ids[:, None] != slot_ids[None, :])
    scores = lax.dot_general(
        arrived, arrived, (((1,), (1,)), ((), ())), preferred_element_type=jnp.float32
    )
    highest = jnp.max(jnp.where(paired, scores, -1e30), axis=1)
    back = highest.reshape(grp_count, wide_count, CAP)
    back = lax.all_to_all(back, "wide", split_axis=1, concat_axis=1, tiled=True)
    back = lax.all_to_all(back, GRP, split_axis=0, concat_axis=0, tiled=True)
    own_best = back.reshape(slot_count)[position]
    return jnp.where(own_best > -1e29, own_best, 0.0)


def z_shift(step):
    return [(z, (z + step) % PLANES) for z in range(PLANES)]


def after(value, *others):
    return lax.optimization_barrier((value,) + others)[0]


def call(kernel, out_shape, flops, **settings):
    return pl.pallas_call(
        kernel,
        out_shape=out_shape,
        compiler_params=pltpu.CompilerParams(vmem_limit_bytes=VMEM_LIMIT),
        cost_estimate=pl.CostEstimate(
            flops=flops, bytes_accessed=8 * 2**20, transcendentals=0
        ),
        **settings,
    )


def whole(value):
    return pl.BlockSpec(value.shape, lambda *_: (0,) * value.ndim)


def columns(rows, tile, first=0):
    return pl.BlockSpec((rows, tile), lambda i: (0, first + i))


def window(rows, tile, first):
    return pl.BlockSpec((pl.Element(rows), pl.Element(tile)), lambda i: (0, pl.multiple_of(first + i * tile, 128)))


def vmem():
    return pl.BlockSpec(memory_space=pltpu.VMEM)


def smem():
    return pl.BlockSpec(memory_space=pltpu.SMEM)


def iota(shape, axis):
    return lax.broadcasted_iota(jnp.int32, shape, axis)


def select_rows(pick, rows):
    return jnp.dot(pick, rows, preferred_element_type=jnp.float32)


def plan_kernel(
    where_ref,
    target_ref,
    x_ref,
    list_ref,
    wide_ref,
    note_ref,
    scale_ref,
    back_ref,
    flag_ref,
    squares,
):
    step = pl.program_id(0)
    f32, bf16 = jnp.float32, jnp.bfloat16
    part = jnp.zeros((HALF, 128), f32)
    for first in range(0, x_ref.shape[1], 128):
        values = x_ref[:, first : first + 128].astype(f32)
        part = part + values * values

    @pl.when(step == 0)
    def _():
        squares[...] = part
        z = where_ref[0]
        target = target_ref[...]
        across = (target == iota((WORKERS, HALF), 0)).astype(bf16)
        earlier = (iota((HALF, HALF), 0) < iota((HALF, HALF), 1)).astype(bf16)
        before = select_rows(across, earlier)
        counts = lax.dot_general(
            jnp.ones((16, HALF), bf16),
            across,
            (((1,), (1,)), ((), ())),
            preferred_element_type=f32,
        )
        down, over = iota((WORKERS, WORKERS), 0), iota((WORKERS, WORKERS), 1)
        same = down // PER_PLANE == over // PER_PLANE
        ahead = select_rows(counts.astype(bf16), (same & (down < over)).astype(bf16))[0:1, :]
        counts = counts[0:1, :]
        across = across.astype(f32)
        counts_down = jnp.sum(across, axis=1, keepdims=True)
        ahead_down = select_rows(
            (same & (over < down)).astype(bf16),
            jnp.broadcast_to(counts_down, (WORKERS, 128)).astype(bf16),
        )[:, 0:1]
        rank = jnp.sum(across * before, axis=0, keepdims=True).astype(jnp.int32)
        place = jnp.sum(across * (before + ahead_down), axis=0, keepdims=True).astype(jnp.int32)
        distance = (target // PER_PLANE - z) & (PLANES - 1)
        cluster_distance = (iota((1, WORKERS), 1) // PER_PLANE - z) & (PLANES - 1)
        n = [
            jnp.sum(jnp.where(cluster_distance == d, counts, 0.0), axis=1, keepdims=True).astype(
                jnp.int32
            )
            for d in range(PLANES)
        ]
        low = functools.reduce(
            jnp.maximum,
            (
                jnp.zeros_like(n[4]),
                n[4] - CAPS[3] + 1,
                n[4] + n[5] - CAPS[2] + 1,
                n[4] + n[5] + n[6] - CAPS[1] + 1,
                n[4] + n[5] + n[6] + n[7] - CAPS[0] + 1,
            ),
        )
        high = functools.reduce(
            jnp.minimum,
            (
                n[4],
                jnp.full_like(n[4], CAPS[3] - 1),
                CAPS[2] - 1 - n[3],
                CAPS[1] - 1 - n[3] - n[2],
                CAPS[0] - 1 - n[3] - n[2] - n[1],
            ),
        )
        to_right = jnp.clip((low + high) >> 1, 0, n[4])
        starts = [
            None,
            to_right + n[3] + n[2],
            to_right + n[3],
            to_right,
            to_right,
            n[4] - to_right,
            n[4] - to_right + n[5],
            n[4] - to_right + n[5] + n[6],
        ]

        def by_distance(which):
            value = jnp.zeros(which.shape, jnp.int32)
            for d in range(1, PLANES):
                value = jnp.where(which == d, starts[d], value)
            return value

        start = by_distance(distance)
        far_right = (distance == 4) & (place < to_right)
        far_left = (distance == 4) & (place >= to_right)
        goes_right = ((distance >= 1) & (distance <= 3)) | far_right
        on_list = jnp.where(far_right, place, jnp.where(far_left, place - to_right, start + place))
        list_place = jnp.where(
            distance == 0,
            2 * LIST + place,
            jnp.where(
                on_list >= LIST - 1, -1, jnp.where(goes_right, 1 + on_list, LIST + 1 + on_list)
            ),
        )
        list_ref[...] = list_place
        wide_place = (target // WIDE % 2) * HALF + target % WIDE * 32 + distance * CAP + rank
        wide_ref[...] = wide_place
        note_ref[...] = jnp.zeros((1, NOTE), f32)
        note_ref[:, 0:WORKERS] = counts
        note_ref[:, WORKERS : 2 * WORKERS] = ahead
        note_ref[:, 2 * WORKERS : 3 * WORKERS] = by_distance(cluster_distance).astype(f32)
        back_ref[...] = target * CAP + rank
        flag_ref[...] = jnp.broadcast_to((low > high).astype(f32), (1, 128))

    @pl.when(step > 0)
    def _():
        squares[...] += part

    @pl.when(step == pl.num_programs(0) - 1)
    def _():
        features = pl.num_programs(0) * x_ref.shape[1]
        spread = jnp.sum(squares[...], axis=1, keepdims=True) * (1.0 / features)
        scale_ref[...] = lax.rsqrt(spread + 1e-06) * features ** (-0.25)


def plan(where, targets, embeddings):
    f32 = jnp.float32
    shapes = [
        jax.ShapeDtypeStruct((1, HALF), jnp.int32),
        jax.ShapeDtypeStruct((1, HALF), jnp.int32),
        jax.ShapeDtypeStruct((1, NOTE), f32),
        jax.ShapeDtypeStruct((HALF, 1), f32),
        jax.ShapeDtypeStruct((1, HALF), jnp.int32),
        jax.ShapeDtypeStruct((1, 128), f32),
    ]
    return call(
        plan_kernel,
        shapes,
        10**9,
        grid=(4,),
        in_specs=[smem(), whole(targets), columns(HALF, embeddings.shape[1] // 4)],
        out_specs=[whole(shape) for shape in shapes],
        scratch_shapes=[pltpu.VMEM((HALF, 128), f32)],
    )(where, targets, embeddings)


def scaled_rows(x_ref, scale_ref):
    return (x_ref[...].astype(jnp.float32) * scale_ref[...]).astype(jnp.bfloat16)


def pack_lists_kernel(place_ref, note_ref, scale_ref, x_ref, right_ref, left_ref, own_ref, pick):
    @pl.when(pl.program_id(0) == 0)
    def _():
        pick[...] = (iota(pick.shape, 0) == place_ref[...]).astype(jnp.bfloat16)

    packed = select_rows(pick[...], scaled_rows(x_ref, scale_ref))
    first = iota((LIST, 1), 0) == 0
    note = note_ref[...]
    right_ref[...] = jnp.where(first, note, packed[0:LIST, :]).astype(jnp.bfloat16)
    left_ref[...] = jnp.where(first, note, packed[LIST : 2 * LIST, :]).astype(jnp.bfloat16)
    own_ref[...] = packed[2 * LIST :, :].astype(jnp.bfloat16)


def pack_lists(place, note, scale, embeddings, first_column, width):
    tile = width // 2
    parts = (LIST, LIST, OWN_LIST)
    return call(
        pack_lists_kernel,
        [jax.ShapeDtypeStruct((rows, width), jnp.bfloat16) for rows in parts],
        2 * sum(parts) * HALF * width,
        grid=(width // tile,),
        in_specs=[
            whole(place),
            columns(1, tile),
            whole(scale),
            window(HALF, tile, first_column),
        ],
        out_specs=[columns(rows, tile) for rows in parts],
        scratch_shapes=[pltpu.VMEM((sum(parts), HALF), jnp.bfloat16)],
    )(place, note, scale, embeddings)


def pack_wide_kernel(place_ref, scale_ref, x_ref, out_ref, pick, fill):
    @pl.when(pl.program_id(0) == 0)
    def _():
        match = (iota(pick.shape, 0) == place_ref[...]).astype(jnp.float32)
        pick[...] = match.astype(jnp.bfloat16)
        fill[...] = MARK * (1.0 - jnp.sum(match, axis=1, keepdims=True))

    packed = select_rows(pick[...], scaled_rows(x_ref, scale_ref))
    out_ref[...] = (packed + fill[...]).astype(jnp.bfloat16)


def pack_wide(place, scale, embeddings, first_column, width):
    tile = width // 2
    return call(
        pack_wide_kernel,
        jax.ShapeDtypeStruct((OUT, width), jnp.bfloat16),
        2 * OUT * HALF * width,
        grid=(width // tile,),
        in_specs=[
            whole(place),
            whole(scale),
            window(HALF, tile, first_column),
        ],
        out_specs=columns(OUT, tile),
        scratch_shapes=[
            pltpu.VMEM((OUT, HALF), jnp.bfloat16),
            pltpu.VMEM((OUT, 1), jnp.float32),
        ],
    )(place, scale, embeddings)


def reorder_kernel(pick_ref, x_ref, *out_refs):
    moved = select_rows(pick_ref[...], x_ref[...]).astype(jnp.bfloat16)
    for index, out_ref in enumerate(out_refs):
        out_ref[...] = moved[index * 128 : index * 128 + 128, :]


def reorder(pick, value):
    width = value.shape[1]
    tile = 256
    return call(
        reorder_kernel,
        [jax.ShapeDtypeStruct((128, width), jnp.bfloat16)] * PLANES,
        2 * OUT * OUT * width,
        grid=(width // tile,),
        in_specs=[whole(pick), columns(OUT, tile)],
        out_specs=[columns(128, tile)] * PLANES,
    )(pick, value)


def slots_kernel(where_ref, note_ref, *refs):
    firsts, out_ref, told = refs[:-2], refs[-2], refs[-1]
    told[...] = jnp.zeros(told.shape, jnp.float32)
    told[0:1, :] = note_ref[...]
    for index, first in enumerate(firsts):
        told[index + 1 : index + 2, :] = first[...].astype(jnp.float32)[0:1, :]
    slot = iota((OUT, 1), 0)
    step, rank = slot // CAP % PLANES, slot % CAP
    by_step = (iota((OUT, 16), 1) == step).astype(jnp.bfloat16)
    mine = iota((OUT, WORKERS), 1) == where_ref[0] * PER_PLANE + slot // 32

    def heard(index):
        told_here = told[:, index * WORKERS : index * WORKERS + WORKERS].astype(jnp.bfloat16)
        value = jnp.where(mine, select_rows(by_step, told_here), 0.0)
        return jnp.sum(value, axis=1, keepdims=True).astype(jnp.int32)

    count, place, start = heard(0), heard(1) + rank, heard(2)
    offsets = [OWN_LIST]
    for cap in CAPS + CAPS:
        offsets.append(offsets[-1] + cap)
    found = jnp.where(
        place < start, offsets[3] + 1 + place, offsets[7] + 1 + place - start
    )
    for d, block in ((1, 0), (2, 1), (3, 2), (5, 6), (6, 5), (7, 4)):
        found = jnp.where(step == d, offsets[block] + 1 + start + place, found)
    found = jnp.where(step == 0, place, found)
    found = jnp.where(rank < count, found, -1)
    out_ref[...] = (found == iota(out_ref.shape, 1)).astype(jnp.bfloat16)


def slots(where, note, blocks):
    firsts = [blocks[b] for b in (0, 1, 2, 3, 6, 5, 4)]
    shape = jax.ShapeDtypeStruct((OUT, OWN_LIST + 2 * sum(CAPS)), jnp.bfloat16)
    return call(
        slots_kernel,
        shape,
        10**9,
        grid=(1,),
        in_specs=[smem(), whole(note)]
        + [pl.BlockSpec((16, NOTE), lambda i: (0, 0)) for _ in firsts],
        out_specs=whole(shape),
        scratch_shapes=[pltpu.VMEM((16, NOTE), jnp.float32)],
    )(where, note, *firsts)


def repack_kernel(turn, pick_ref, *refs):
    blocks, out_ref, held = refs[:-2], refs[-2], refs[-1]
    step = pl.program_id(0)
    for chunk in range(2):

        @pl.when((step >= turn) == bool(chunk))
        def _(chunk=chunk):
            first = pl.multiple_of((step - chunk * turn) * 256, 256)
            base = 0
            for block in blocks[chunk * 9 : chunk * 9 + 9]:
                rows = block.shape[0]
                held[base : base + rows, :] = block[:, pl.ds(first, 256)]
                base += rows

    out_ref[...] = select_rows(pick_ref[...], held[...]).astype(jnp.bfloat16)


def repack(pick, first_blocks, second_blocks):
    tile = 256
    depth = pick.shape[1]
    turn = first_blocks[0].shape[1] // tile
    steps = turn + second_blocks[0].shape[1] // tile
    blocks = list(first_blocks) + list(second_blocks)
    return call(
        functools.partial(repack_kernel, turn),
        jax.ShapeDtypeStruct((OUT, steps * tile), jnp.bfloat16),
        2 * OUT * depth * steps * tile,
        grid=(steps,),
        in_specs=[whole(value) for value in [pick] + blocks],
        out_specs=columns(OUT, tile),
        scratch_shapes=[pltpu.VMEM((depth, tile), jnp.bfloat16)],
    )(pick, *blocks)


def gram_kernel(pick_ref, x_ref, out_ref, held):
    step = pl.program_id(0)
    held[step] = select_rows(pick_ref[...], x_ref[...]).astype(jnp.bfloat16)

    @pl.when(step == pl.num_programs(0) - 1)
    def _():
        for tile in range(0, OUT, ROW_TILE):
            part = 0.0
            for index in range(held.shape[0]):
                part = part + lax.dot_general(
                    held[index, tile : tile + ROW_TILE, :],
                    held[index, tile:, :],
                    (((1,), (1,)), ((), ())),
                    preferred_element_type=jnp.float32,
                )
            out_ref[tile : tile + ROW_TILE, tile:] = part


def gram(pick, value):
    width = value.shape[1]
    tile = 768
    return call(
        gram_kernel,
        jax.ShapeDtypeStruct((OUT, OUT), jnp.float32),
        4 * OUT * OUT * width,
        grid=(width // tile,),
        in_specs=[whole(pick), columns(OUT, tile)],
        out_specs=pl.BlockSpec((OUT, OUT), lambda i: (0, 0)),
        scratch_shapes=[pltpu.VMEM((width // tile, OUT, tile), jnp.bfloat16)],
    )(pick, value)


def best_kernel(where_ref, flag_ref, total_ref, *refs):
    blocks, out_ref, held = refs[:PLANES], refs[PLANES], refs[-1]
    for index, block in enumerate(blocks):
        held[index * 128 : index * 128 + 128, :] = block[...]
    count = OUT // ROW_TILE
    same = iota((ROW_TILE, ROW_TILE), 0) == iota((ROW_TILE, ROW_TILE), 1)
    best = [jnp.full((1, ROW_TILE), -1e30, jnp.float32)] * count
    filled = [None] * count
    for tile in reversed(range(count)):
        first = tile * ROW_TILE
        part = total_ref[first : first + ROW_TILE, first:] + lax.dot_general(
            held[first : first + ROW_TILE, :],
            held[first:, :],
            (((1,), (1,)), ((), ())),
            preferred_element_type=jnp.float32,
        )
        diagonal = jnp.where(same, part[:, :ROW_TILE], 0.0)
        row_filled = jnp.sum(diagonal, axis=1, keepdims=True) < REAL_MAX
        filled[tile] = jnp.sum(diagonal, axis=0, keepdims=True) < REAL_MAX
        across = jnp.full((ROW_TILE, 1), -1e30, jnp.float32)
        for other in range(tile, count):
            scores = part[:, (other - tile) * ROW_TILE : (other - tile + 1) * ROW_TILE]
            allowed = row_filled & jnp.logical_not(same) if other == tile else row_filled
            down = jnp.max(jnp.where(allowed, scores, -1e30), axis=0, keepdims=True)
            best[other] = jnp.maximum(best[other], down)
            if other > tile:
                most = jnp.max(jnp.where(filled[other], scores, -1e30), axis=1, keepdims=True)
                across = jnp.maximum(across, most)
        turned = jnp.sum(jnp.where(same, across, 0.0), axis=0, keepdims=True)
        best[tile] = jnp.maximum(best[tile], turned)
    for d in range(PLANES):
        result = best[d // 2][:, d % 2 * 128 : d % 2 * 128 + 128]
        result = jnp.where(result > -1e29, result, 0.0)
        result = jnp.where(flag_ref[0:1, 0:1] > 0.5, 1e30, result)
        plane = (where_ref[0] - d) & (PLANES - 1)
        out_ref[pl.ds(pl.multiple_of(plane * 32, 32), 32), :] = jnp.broadcast_to(
            result, (32, 128)
        )


def best_of(where, flag, total, blocks):
    width = blocks[0].shape[1]
    shape = jax.ShapeDtypeStruct((WORKERS, 128), jnp.float32)
    return call(
        best_kernel,
        shape,
        2 * OUT * OUT * width,
        grid=(1,),
        in_specs=[smem()] + [whole(value) for value in [flag, total] + blocks],
        out_specs=whole(shape),
        scratch_shapes=[pltpu.VMEM((OUT, width), jnp.bfloat16)],
    )(where, flag, total, *blocks)


def on_device(embeddings, worker_of_row):
    i32 = jnp.int32
    core = lax.axis_index("core")
    wide = lax.axis_index("wide")
    where = lax.axis_index("z").astype(i32).reshape(1)
    list_place, wide_place, note, scale, back_place, flag = plan(
        where, worker_of_row.reshape(1, HALF), embeddings
    )

    packed, own = [], []
    for f in range(2):
        right, left, mine = pack_lists(
            list_place, note, scale, embeddings, sum(Z_FIRST[:f]), Z_FIRST[f]
        )
        packed.append((right, left))
        own.append(mine)

    wide_rows = pack_wide(
        after(wide_place, packed[0][0]), scale, embeddings, sum(Z_FIRST), WIDE_FIRST
    )
    wide_back = lax.all_to_all(wide_rows, CORE_WIDE, 0, 0, tiled=True)

    slot_ids = jnp.arange(OUT, dtype=i32)
    final = slot_ids[:, None]
    step_of, core_of, column_of = final // 128, final // 64 % 2, final // 4 % WIDE
    final_from = core_of * HALF + column_of * 32 + step_of * CAP + final % CAP
    final_order = (final_from == slot_ids[None, :]).astype(jnp.bfloat16)

    got = [([], []), ([], [])]
    for hop in range(4):
        if hop == 2:
            blocks = reorder(after(final_order, got[0][0][1]), wide_back)
        for f in range(2):
            for side, steps in enumerate((z_shift(1), z_shift(-1))):
                if hop == 0:
                    block = packed[f][side]
                else:
                    block = got[f][side][-1][: CAPS[hop]]
                if hop == 1:
                    block = after(block, wide_rows)
                if hop == 2 and f == 1:
                    block = after(block, blocks[1])
                got[f][side].append(lax.ppermute(block, "z", steps))
    got = [rights + lefts for rights, lefts in got]
    last = [blocks[0]] + [None] * 7
    for steps, gate in (((4,), ()), ((1, 7, 2, 6), (4,)), ((3, 5), (1, 7))):
        for step in steps:
            block = blocks[step]
            if gate:
                block = after(block, *[last[done] for done in gate])
            last[step] = lax.ppermute(block, "z", z_shift(step))

    slot_pick = slots(where, note, got[0])
    packed = repack(slot_pick, [own[0]] + got[0], [own[1]] + got[1])
    packed = after(packed, wide_back, last[4])
    arrived = lax.all_to_all(packed, CORE_WIDE, 0, 0, tiled=True)
    best = best_of(where, flag, gram(final_order, arrived), last)

    back = lax.all_to_all(best, ALL, 0, 0, tiled=True)
    mine = lax.dynamic_slice(back, (0, core * 64 + wide * CAP), (WORKERS, CAP))
    failed = jnp.max(mine) > 1e29
    result = jnp.sum(
        jnp.where(back_place == slot_ids[:, None], mine.reshape(OUT)[:, None], 0.0), axis=0
    )
    return lax.cond(failed, padded_plan, lambda *_: result, embeddings, worker_of_row)


def solution(mesh):
    split = jax.sharding.Mesh(mesh.devices.reshape(PLANES, 2, WIDE), ALL)
    placed = (P(ALL, None), P(ALL, None))
    return jax.shard_map(
        on_device, mesh=split, in_specs=placed, out_specs=P(ALL), check_vma=False
    )
```
